512 devices in a mesh: frame: 32 (over x, y_lo, core), patch: 16 (over y_hi, z).
Axes of the slice: x: 4, y: 8 (y_hi: 2, y_lo: 4; y = y_hi * 4 + y_lo), z: 8, core: 2. Of those that a mesh axis runs over, the one named last changes fastest.
Arguments:
- latents: bfloat16 [32, 48, 128, 320], P('frame', 'patch'), may hold values from -6 to 6
- stale_kv: bfloat16 [32, 48, 128, 640], P('frame', 'patch'), may hold values from -8 to 8
- frame_ids: int32 [32], replicated, may hold values from 0 to 63
- timestep: int32 [1], replicated, may hold values from 0 to 999
- conv_weight: bfloat16 [3, 3, 320, 320], replicated, may hold values from -0.109375 to 0.109375
- time_proj: bfloat16 [320, 320], replicated, may hold values from -0.3125 to 0.3125
- spatial_qkv: bfloat16 [320, 960], replicated, may hold values from -0.4472136 to 0.4472136
- spatial_out: bfloat16 [320, 320], replicated, may hold values from -0.3125 to 0.3125
- temporal_qkv: bfloat16 [320, 960], replicated, may hold values from -0.3125 to 0.3125
- temporal_out: bfloat16 [320, 320], replicated, may hold values from -0.3125 to 0.3125
- frame_table: bfloat16 [64, 320], replicated, may hold values from -6 to 6
Outputs:
- result: bfloat16 [32, 48, 128, 320], P('frame', 'patch')
- fresh_kv: bfloat16 [32, 48, 128, 640], P('frame', 'patch')
The draws below stay inside these ranges and needn't reach their ends.
All inputs are finite; a program needn't handle non-finite values.
Results may differ from the reference program's by a relative error of at most 0.011.
Values may be sent and summed in bfloat16 or wider, within the bound.
A program may use at most 64 MiB of HBM per device.

```python
import math
import jax
import jax.numpy as jnp
from jax import lax

C = 320
HEADS = 5
HEAD_DIM = 64
GROUPS = 32
NPOS = 64
STEPS = 1000
ROWS_DEV = 3
LAT_W = 128
LAT_H = 48
FRAMES = 32
N_PATCH = 16


def draw_stale_kv(key, part):
    key = jax.random.fold_in(key, 11)
    shape = (FRAMES, LAT_H, LAT_W, 2 * C)
    scales = jnp.concatenate([jnp.full((C,), 1.5, jnp.float32), jnp.full((C,), 2.0, jnp.float32)])
    base = jax.random.truncated_normal(key, -4.0, 4.0, shape, jnp.float32)
    return (base * scales).astype(jnp.bfloat16)


def draw_spatial_qkv(key, part):
    key = jax.random.fold_in(key, 23)
    base = jax.random.truncated_normal(key, -3.96, 3.96, (C, 3 * C), jnp.float32)
    scales = jnp.concatenate([jnp.full((2 * C,), 1.5, jnp.float32), jnp.full((C,), 2.0, jnp.float32)])
    return (base * scales / math.sqrt(C)).astype(jnp.bfloat16)


def with_ends(values, key, low, high):
    spot = [jax.random.randint(jax.random.fold_in(key, axis), (), 0, length) for axis, length in enumerate(values.shape)]
    longest = values.shape.index(max(values.shape))
    beside = spot[:longest] + [(spot[longest] + 1) % values.shape[longest]] + spot[longest + 1:]
    return values.at[tuple(spot)].set(low).at[tuple(beside)].set(high)


def steps_of(stream_key, dims, cuts, low, top_value):
    factor_of = 1.0
    for dim, parts in cuts:
        draws = jax.random.uniform(jax.random.fold_in(jax.random.fold_in(stream_key, 6), dim), (parts,), jnp.float32, low / len(cuts), top_value / len(cuts))
        factor_of = factor_of * jnp.repeat(jnp.exp(draws), dims[dim] // parts).reshape((-1,) + (1,) * (len(dims) - 1 - dim))
    return factor_of


def scatter_about(rng, dims, width, reach, cuts=(), kind=jnp.bfloat16):
    factor_of = steps_of(rng, dims, cuts, -0.22, 0.18) if cuts else 1.0
    entries = jax.random.normal(rng, dims, jnp.float32) * width * factor_of
    return jnp.minimum(jnp.maximum(entries, -reach), reach).astype(kind)


def setup_inputs(seed: int = 0) -> dict:
    seeds = jax.random.split(jax.random.key(seed), 12)
    return {
        "latents": scatter_about(seeds[0], (FRAMES, LAT_H, LAT_W, C), 1.0, 6.0, ((0, 32), (1, 16))),
        "stale_kv": draw_stale_kv(jax.random.fold_in(seeds[11], 71), 0),
        "frame_ids": with_ends(jax.random.randint(seeds[2], (FRAMES,), 0, NPOS), jax.random.fold_in(seeds[2], 1), 0, NPOS - 1).astype(jnp.int32),
        "timestep": jax.random.randint(seeds[3], (1,), 0, STEPS).astype(jnp.int32),
        "conv_weight": scatter_about(seeds[4], (3, 3, C, C), (9 * C) ** -0.5, 0.109375),
        "time_proj": scatter_about(seeds[5], (C, C), C ** -0.5, 0.3125),
        "spatial_qkv": draw_spatial_qkv(jax.random.fold_in(seeds[11], 71), 0),
        "spatial_out": scatter_about(seeds[7], (C, C), C ** -0.5, 0.3125),
        "temporal_qkv": scatter_about(seeds[8], (C, 3 * C), C ** -0.5, 0.3125),
        "temporal_out": scatter_about(seeds[9], (C, C), C ** -0.5, 0.3125),
        "frame_table": scatter_about(seeds[10], (NPOS, C), 1.0, 6.0),
    }


def layer_norm(values):
    centre = values - lax.optimization_barrier(jnp.mean(values, axis=-1, keepdims=True))
    spread = lax.optimization_barrier(jnp.mean(centre * centre, axis=-1, keepdims=True))
    return centre * lax.rsqrt(spread + 1e-05)

def rounded(values):
    return lax.optimization_barrier(values.astype(jnp.bfloat16)).astype(jnp.float32)

def time_bias(timestep, time_proj):
    half = C // 2
    freqs = jnp.exp(-math.log(10000.0) * jnp.arange(half, dtype=jnp.float32) / half)
    angles = timestep[0].astype(jnp.float32) * freqs
    emb = jnp.concatenate([jnp.cos(angles), jnp.sin(angles)]).astype(jnp.bfloat16)
    return jnp.dot(emb[None], time_proj, preferred_element_type=jnp.float32)[0]

def attention(queries, keys, values):
    count = queries.shape[0]
    qh = queries.astype(jnp.float32).reshape(count, HEADS, HEAD_DIM)
    kh = keys.astype(jnp.float32).reshape(keys.shape[0], HEADS, HEAD_DIM)
    vh = values.astype(jnp.float32).reshape(values.shape[0], HEADS, HEAD_DIM)
    scores = jnp.einsum('qhd,khd->hqk', qh, kh) / math.sqrt(HEAD_DIM)
    peak = lax.optimization_barrier(jnp.max(scores, axis=-1, keepdims=True))
    weights = jnp.exp(scores - peak)
    total = lax.optimization_barrier(jnp.sum(weights, axis=-1))
    summed = jnp.einsum('hqk,khd->qhd', rounded(weights), vh)
    return (summed / jnp.transpose(total)[:, :, None]).reshape(count, C).astype(jnp.bfloat16)

def frame_section(latent, stale, bias, conv_weight, spatial_qkv, spatial_out):
    tokens = LAT_H * LAT_W
    values = latent.astype(jnp.float32)
    grouped = values.reshape(tokens, GROUPS, C // GROUPS)
    mean = lax.optimization_barrier(jnp.mean(grouped, axis=(0, 2)))
    var = lax.optimization_barrier(jnp.mean(grouped * grouped, axis=(0, 2))) - mean * mean
    normed = (grouped - mean[None, :, None]) * lax.rsqrt(var + 1e-05)[None, :, None]
    act = jax.nn.silu(normed).astype(jnp.bfloat16).reshape(LAT_H, LAT_W, C)
    padded = jnp.pad(act, ((1, 1), (1, 1), (0, 0)))
    conv = jnp.zeros((tokens, C), jnp.float32)
    for row_step in range(3):
        for col_step in range(3):
            window = padded[row_step:row_step + LAT_H, col_step:col_step + LAT_W].reshape(tokens, C)
            conv = conv + jnp.dot(window, conv_weight[row_step, col_step], preferred_element_type=jnp.float32)
    hidden1 = values.reshape(tokens, C) + conv + bias[None]
    norm1 = layer_norm(hidden1).astype(jnp.bfloat16)
    projected = jnp.dot(norm1, spatial_qkv, preferred_element_type=jnp.float32).astype(jnp.bfloat16)
    queries = projected[:, :C]
    fresh = projected[:, C:]
    older = stale.reshape(tokens, 2 * C)
    row_patch = jnp.repeat(jnp.arange(LAT_H, dtype=jnp.int32) // ROWS_DEV, LAT_W)
    block = ROWS_DEV * LAT_W

    def per_patch(patch_index):
        own_queries = lax.dynamic_slice_in_dim(queries, (patch_index * block).astype(jnp.int32), block, 0)
        mixed = jnp.where((row_patch == patch_index)[:, None], fresh, older)
        return attention(own_queries, mixed[:, :C], mixed[:, C:])
    spatial = lax.map(per_patch, jnp.arange(N_PATCH, dtype=jnp.int32)).reshape(tokens, C)
    hidden2 = hidden1 + jnp.dot(spatial, spatial_out, preferred_element_type=jnp.float32)
    return (hidden2.astype(jnp.bfloat16), fresh)

def reference(latents, stale_kv, frame_ids, timestep, conv_weight, time_proj, spatial_qkv, spatial_out, temporal_qkv, temporal_out, frame_table):
    bias = time_bias(timestep, time_proj)

    def one_frame(pair):
        return frame_section(pair[0], pair[1], bias, conv_weight, spatial_qkv, spatial_out)
    hidden2, fresh = lax.map(one_frame, (latents, stale_kv))
    onehot = (frame_ids[:, None] == jnp.arange(NPOS, dtype=jnp.int32)[None, :]).astype(jnp.bfloat16)
    position = jnp.dot(onehot, frame_table, preferred_element_type=jnp.float32)
    blocks = LAT_H
    stacked = jnp.transpose(hidden2.reshape(FRAMES, blocks, LAT_W, C), (1, 0, 2, 3))

    def temporal_block(feature):
        base = feature.astype(jnp.float32)
        shifted = base + position[:, None, :]
        norm2 = layer_norm(shifted).astype(jnp.bfloat16).reshape(FRAMES * LAT_W, C)
        projected = jnp.dot(norm2, temporal_qkv, preferred_element_type=jnp.float32).astype(jnp.bfloat16)
        projected = projected.astype(jnp.float32).reshape(FRAMES, LAT_W, 3, HEADS, HEAD_DIM)
        query = projected[:, :, 0]
        key = projected[:, :, 1]
        value = projected[:, :, 2]
        scores = jnp.einsum('ftha,gtha->thfg', query, key) / math.sqrt(HEAD_DIM)
        peak = lax.optimization_barrier(jnp.max(scores, axis=-1, keepdims=True))
        weights = jnp.exp(scores - peak)
        total = lax.optimization_barrier(jnp.sum(weights, axis=-1))
        summed = jnp.einsum('thfg,gtha->ftha', rounded(weights), value)
        mixed = (summed / jnp.transpose(total, (2, 0, 1))[..., None]).reshape(FRAMES * LAT_W, C).astype(jnp.bfloat16)
        out = base.reshape(FRAMES * LAT_W, C) + jnp.dot(mixed, temporal_out, preferred_element_type=jnp.float32)
        return out.astype(jnp.bfloat16).reshape(FRAMES, LAT_W, C)
    result = lax.map(temporal_block, stacked)
    result = jnp.transpose(result, (1, 0, 2, 3))
    return (result, fresh.reshape(FRAMES, LAT_H, LAT_W, 2 * C))
```

```python
import functools
import math

import jax
import jax.numpy as jnp
from jax import lax
from jax.experimental import pallas as pl
from jax.experimental.pallas import tpu as pltpu
from jax.sharding import PartitionSpec as P

HEADS = 5
GROUPS = 32
F32 = jnp.float32
BF16 = jnp.bfloat16
MESH = pl.DeviceIdType.MESH
LOG2E = math.log2(math.e)
HIGHEST = lax.Precision.HIGHEST

STAGES = (((1, 2, True), (1, 2, False), (0, 0, False)), ((0, 1, True), (0, 1, False)))
FIRST = (0, 3)
FRESH = 8
STEPS = (
    (0, 0, FRESH, 1),
    (1, 0, FRESH, 1),
    (0, 0, 1, 2),
    (1, 0, 1, 2),
    (0, 0, 3, 2),
    (1, 0, 3, 2),
    (0, 1, 0, 1),
    (0, 1, 1, 2),
    (0, 1, 3, 2),
    (0, 1, 5, 2),
    (1, 1, 0, 1),
    (1, 1, 1, 2),
    (0, 1, 7, 1),
    (1, 1, 3, 2),
    (0, 0, 5, 2),
    (1, 1, 5, 2),
    (0, 0, 7, 1),
    (1, 1, 7, 1),
    (1, 0, 5, 2),
    (1, 0, 7, 1),
)


def iota(shape, dim):
    return lax.broadcasted_iota(jnp.int32, shape, dim)


def dot(a, b, precision=None):
    return lax.dot_general(
        a, b, (((1,), (0,)), ((), ())), preferred_element_type=F32, precision=precision
    )


def dot_nt(a, b, precision=None):
    return lax.dot_general(
        a, b, (((1,), (1,)), ((), ())), preferred_element_type=F32, precision=precision
    )


def layer_norm(values):
    centre = values - jnp.mean(values, axis=-1, keepdims=True)
    spread = jnp.mean(centre * centre, axis=-1, keepdims=True)
    return centre * lax.rsqrt(spread + 1e-05)


def group_of_channel(chans):
    per_group = chans // GROUPS
    chan = iota((chans, 128), 0)
    group = iota((chans, 128), 1)
    inside = (chan >= group * per_group) & (chan < (group + 1) * per_group)
    return jnp.where(inside, 1.0, 0.0).astype(F32)


def from_step(i, k):
    return lax.div(i - k + 32, 32)


def lookup(i, values):
    out = values[0]
    for k in range(1, len(values)):
        if values[k] != values[k - 1]:
            out = out + (values[k] - values[k - 1]) * from_step(i, k)
    return out


def kernel(
    rows,
    width,
    chans,
    lat_in,
    stale_in,
    time_ref,
    conv_in,
    tproj_in,
    qkv_in,
    wout_in,
    ids_in,
    table_in,
    tqkv_in,
    tout_in,
    res_out,
    fresh_out,
    lat_t,
    stale_v,
    conv_w,
    tproj_v,
    qkv_v,
    wout_v,
    ids_v,
    table_v,
    tqkv_v,
    tout_v,
    lat,
    kv_a,
    kv_b,
    halo,
    act,
    stat_out,
    stat_in,
    hidden1,
    wq,
    fresh_v,
    qbuf_a,
    qbuf_b,
    qmask,
    peak,
    acc,
    obuf_a,
    obuf_b,
    lse_a,
    lse_b,
    hid,
    position,
    other,
    twq,
    gathered,
    proj,
    done,
    load_sem,
    halo_send,
    halo_recv,
    stat_send,
    stat_recv,
    ring_send,
    ring_recv,
    part_send,
    part_recv,
    own_sem,
    out_send,
    out_recv,
    back_send,
    back_recv,
):
    block = rows * width
    half = block // 2
    me = lax.axis_index("patch")
    n_patch = lax.axis_size("patch")
    ring = n_patch // 2
    z = lax.rem(me, ring)
    base_z = me - z
    right = base_z + lax.rem(z + 1, ring)
    left = base_z + lax.rem(z + ring - 1, ring)
    partner = lax.rem(me + ring, n_patch)
    frame = lax.axis_index("frame")
    frames = lax.axis_size("frame")
    kv = (kv_a, kv_b)
    qbuf = (qbuf_a, qbuf_b)


    loads = [
        pltpu.make_async_copy(src, dst, load_sem.at[i])
        for i, (src, dst) in enumerate(
            (
                (stale_in, stale_v),
                (lat_in, lat_t),
                (tproj_in, tproj_v),
                (conv_in, conv_w),
                (qkv_in, qkv_v),
                (wout_in, wout_v),
                (ids_in, ids_v),
                (table_in, table_v),
                (tqkv_in, tqkv_v),
                (tout_in, tout_v),
            )
        )
    ]
    (
        load_stale,
        load_lat,
        load_tproj,
        load_conv,
        load_qkv,
        load_wout,
        load_ids,
        load_table,
        load_tqkv,
        load_tout,
    ) = loads

    def ring_copy(stage, direction, i):
        dist = i // 2 + 1
        part = i % 2 if direction == 0 else 1 - i % 2
        window = pl.ds(part * half, half)
        dst_slot = 7 if dist == 4 else 2 * dist - 1 + direction
        src_slot = 0 if dist == 1 else 2 * dist - 3 + direction
        return pltpu.make_async_remote_copy(
            src_ref=kv[stage].at[src_slot, window],
            dst_ref=kv[stage].at[dst_slot, window],
            send_sem=ring_send.at[stage, direction, i],
            recv_sem=ring_recv.at[stage, direction, i],
            device_id={"patch": right if direction == 0 else left},
            device_id_type=MESH,
        )

    def ring_start(stage):
        for i in range(2):
            for direction in range(2):
                ring_copy(stage, direction, i).start()

    def ring_wait(stage, e):
        for direction in range(2):
            ring_copy(stage, direction, e).wait_recv()

    def ring_forward(stage, e):
        for direction in range(2):
            ring_copy(stage, direction, e + 2).start()

    def ring_event(stage, e):
        for direction in range(2):
            ring_copy(stage, direction, e).wait_recv()
            if e + 2 < 7:
                ring_copy(stage, direction, e + 2).start()

    def halo_copy(direction):
        window = pl.ds((rows - 1) * width, width) if direction == 0 else pl.ds(0, width)
        return pltpu.make_async_remote_copy(
            src_ref=lat.at[window],
            dst_ref=halo.at[direction],
            send_sem=halo_send.at[direction],
            recv_sem=halo_recv.at[direction],
            device_id={"patch": me + 1 if direction == 0 else me - 1},
            device_id_type=MESH,
        )

    def stat_copy(k):
        return pltpu.make_async_remote_copy(
            src_ref=stat_out,
            dst_ref=stat_in.at[k],
            send_sem=stat_send.at[k],
            recv_sem=stat_recv.at[k],
            device_id={"patch": lax.rem(me + k, n_patch)},
            device_id_type=MESH,
        )

    def part_copy(src, dst, k):
        return pltpu.make_async_remote_copy(
            src_ref=src,
            dst_ref=dst,
            send_sem=part_send.at[k],
            recv_sem=part_recv.at[k],
            device_id={"patch": partner},
            device_id_type=MESH,
        )

    query_copies = [part_copy(qbuf[s].at[0], qbuf[s].at[1], s) for s in range(2)]
    output_copies = [(part_copy(obuf_a.at[0], obuf_a.at[1], 2), part_copy(lse_a.at[0], lse_a.at[1], 3))]
    for c in range(rows):
        window = pl.ds(c * width, width)
        output_copies.append(
            (
                part_copy(obuf_b.at[0, window], obuf_b.at[1, window], 4 + 2 * c),
                part_copy(lse_b.at[0, c], lse_b.at[1, c], 5 + 2 * c),
            )
        )

    def group_rows(g):
        return pl.ds(pl.multiple_of(g * 16, 16), 16)

    per_row = width // 16

    def is_active(f):
        return lax.rem(f, 4) < rows

    def group_of(f):
        return lax.rem(f, 4) * per_row + lax.div(f, 4)

    def out_copy(target):
        return pltpu.make_async_remote_copy(
            src_ref=hid.at[group_rows(group_of(target))],
            dst_ref=gathered.at[group_rows(frame)],
            send_sem=out_send.at[target],
            recv_sem=out_recv.at[frame],
            device_id={"frame": target},
            device_id_type=MESH,
        )

    def back_copy(target):
        return pltpu.make_async_remote_copy(
            src_ref=done.at[group_rows(target)],
            dst_ref=res_out.at[group_rows(group_of(frame))],
            send_sem=back_send.at[target],
            recv_sem=back_recv.at[frame],
            device_id={"frame": target},
            device_id_type=MESH,
        )

    def arrival(source, buffer, rows_of_it, sems):
        return pltpu.make_async_remote_copy(
            src_ref=done.at[pl.ds(0, 16)],
            dst_ref=buffer.at[rows_of_it],
            send_sem=out_send.at[0],
            recv_sem=sems.at[source],
            device_id={"frame": source},
            device_id_type=MESH,
        )


    barrier = pltpu.get_barrier_semaphore()

    def greet_patch(k, carry):
        pl.semaphore_signal(
            barrier,
            inc=1,
            device_id={"patch": lax.rem(me + k, n_patch)},
            device_id_type=MESH,
        )
        return carry

    def greet_frame(k, carry):
        pl.semaphore_signal(
            barrier,
            inc=1,
            device_id={"frame": lax.rem(frame + k, frames)},
            device_id_type=MESH,
        )
        return carry

    lax.fori_loop(1, n_patch, greet_patch, 0)
    lax.fori_loop(1, frames, greet_frame, 0)
    for load in loads:
        load.start()

    low = iota((block, 128), 1) < 64

    def arrange(source, slot):
        kv_a[slot, :, 0:128] = jnp.where(low, source[:, 256:384], source[:, 512:640])
        kv_a[slot, :, 128:256] = source[:, 0:128]
        kv_a[slot, :, 256:384] = source[:, 320:448]
        kv_b[slot, :, 0:128] = source[:, 128:256]
        kv_b[slot, :, 128:256] = source[:, 448:576]

    load_stale.wait()
    arrange(stale_v, 0)
    load_lat.wait()
    for r in range(rows):
        lat[r * width : (r + 1) * width] = lat_t[r].astype(F32).T.astype(BF16)

    pl.semaphore_wait(barrier, n_patch - 1 + frames - 1)
    ring_start(0)

    @pl.when(me < n_patch - 1)
    def _():
        halo_copy(0).start()

    @pl.when(me > 0)
    def _():
        halo_copy(1).start()

    values = lat[...].astype(F32)
    col_sum = jnp.sum(values, axis=0, keepdims=True)
    col_sq = jnp.sum(values * values, axis=0, keepdims=True)
    row8 = iota((8, chans), 0)
    cols = jnp.where(row8 == 0, col_sum, jnp.where(row8 == 1, col_sq, 0.0))
    member = group_of_channel(chans)
    stat_out[...] = dot(cols, member, HIGHEST)

    def send_stat(k, carry):
        stat_copy(k).start()
        return carry

    lax.fori_loop(1, n_patch, send_stat, 0)
    ring_start(1)

    load_tproj.wait()
    lane_c = iota((8, chans), 1)
    half_c = chans // 2
    order = jnp.where(lane_c < half_c, lane_c, lane_c - half_c).astype(F32)
    freqs = jnp.exp(-math.log(10000.0) * order / half_c)
    angles = time_ref[0].astype(F32) * freqs
    emb = jnp.where(lane_c < half_c, jnp.cos(angles), jnp.sin(angles)).astype(BF16)
    bias = dot(emb, tproj_v[...])[0:1]
    load_conv.wait()
    load_qkv.wait()
    wq[...] = jnp.zeros_like(wq)
    wq[:, 0:chans] = qkv_v[:, 0:chans]
    peak[...] = jnp.full(peak.shape, -1e30, F32)
    acc[...] = jnp.zeros(acc.shape, F32)


    def wait_stat(k, carry):
        stat_copy(k).wait_recv()
        return carry

    lax.fori_loop(1, n_patch, wait_stat, 0)
    total = stat_out[...]
    for k in range(1, 16):
        total = total + stat_in[k]
    count = block * (chans // GROUPS) * n_patch
    mean = total[0:1] / count
    var = total[1:2] / count - mean * mean
    rstd = lax.rsqrt(var + 1e-05)
    row8g = iota((8, 128), 0)
    spread = dot_nt(jnp.where(row8g == 0, mean, jnp.where(row8g == 1, rstd, 0.0)), member, HIGHEST)
    mean_c, rstd_c = spread[0:1], spread[1:2]

    def activate(x):
        normed = (x.astype(F32) - mean_c) * rstd_c
        return (normed / (1.0 + jnp.exp(-normed))).astype(BF16)

    act[width : width + block] = activate(lat[...])

    @pl.when(me > 0)
    def _():
        halo_copy(0).wait_recv()
        act[0:width] = activate(halo[0])

    @pl.when(me == 0)
    def _():
        act[0:width] = jnp.zeros((width, chans), BF16)

    @pl.when(me < n_patch - 1)
    def _():
        halo_copy(1).wait_recv()
        act[width + block :] = activate(halo[1])

    @pl.when(me == n_patch - 1)
    def _():
        act[width + block :] = jnp.zeros((width, chans), BF16)

    ring_event(0, 0)


    column = iota((block, chans), 0) & (width - 1)

    def conv_column(step):
        out = dot(act[0:block], conv_w[0, step])
        out = out + dot(act[width : width + block], conv_w[1, step])
        return out + dot(act[2 * width : 2 * width + block], conv_w[2, step])

    conv = conv_column(1)
    conv = conv + jnp.where(column == 0, 0.0, pltpu.roll(conv_column(0), 1, 0))
    ring_event(0, 1)
    conv = conv + jnp.where(column == width - 1, 0.0, pltpu.roll(conv_column(2), block - 1, 0))
    h1 = lat[...].astype(F32) + conv + bias
    hidden1[...] = h1
    norm1 = layer_norm(h1).astype(BF16)
    queries = dot(norm1, wq[...]) * (LOG2E / 8.0)
    low_half = iota((half, 128), 1) < 64
    qbuf_a[0, 0:block] = queries[:, 0:128].astype(BF16)
    folded = jnp.where(
        low_half, queries[0:half, 256:384], pltpu.roll(queries[half:, 256:384], 64, 1)
    )
    qbuf_a[0, block:] = folded.astype(BF16)
    query_copies[0].start()
    qbuf_b[0] = queries[:, 128:256].astype(BF16)
    query_copies[1].start()
    ring_event(1, 0)
    ring_event(1, 1)
    fresh_v[...] = dot(norm1, qkv_v[:, chans:]).astype(BF16)
    store_fresh = pltpu.make_async_copy(fresh_v, fresh_out, own_sem.at[2])
    store_fresh.start()
    arrange(fresh_v, FRESH)

    def mask_queries(stage, which):
        def keep(tile, lanes):
            return jnp.where(lanes, tile, jnp.zeros_like(tile))

        if stage == 0:
            tile = qbuf_a[which, 0:block]
            qmask[which, 0] = keep(tile, low)
            qmask[which, 1] = keep(tile, ~low)
            tile = qbuf_a[which, block:].astype(F32)
            qmask[which, 2, 0:half] = jnp.where(low_half, tile, 0.0).astype(BF16)
            tile = pltpu.roll(tile, 64, 1)
            qmask[which, 2, half:] = jnp.where(low_half, tile, 0.0).astype(BF16)
        else:
            tile = qbuf_b[which]
            qmask[which, 3] = keep(tile, low)
            qmask[which, 4] = keep(tile, ~low)

    mask_queries(0, 0)
    mask_queries(1, 0)


    def attend(stage, which, slot, slots):
        heads = STAGES[stage]
        keys = slots * block
        low_keys = iota((keys, 128), 1) < 64

        def tile_of(t):
            return kv[stage][pl.ds(slot, slots), :, t * 128 : t * 128 + 128].reshape(keys, 128)

        def scores_of(j):
            return dot_nt(qmask[which, FIRST[stage] + j], tile_of(heads[j][0]))

        accs = [acc[which, FIRST[stage] + j] for j in range(len(heads))]
        peaks = [peak[which, FIRST[stage] + j] for j in range(len(heads))]
        scores = scores_of(0)
        results = []
        for j, (_, vt, in_low) in enumerate(heads):
            following = scores_of(j + 1) if j + 1 < len(heads) else None
            top = jnp.maximum(peaks[j], jnp.max(scores, axis=1, keepdims=True))
            weights = jnp.exp2(scores - jnp.concatenate([top] * (keys // 128), axis=1))
            vals = tile_of(vt)
            vals = jnp.where(low_keys if in_low else ~low_keys, vals, jnp.ones_like(vals))
            scale = jnp.exp2(peaks[j] - top)
            results.append((accs[j] * scale + dot(weights.astype(BF16), vals), top))
            scores = following
        for j, (new_acc, top) in enumerate(results):
            acc[which, FIRST[stage] + j] = new_acc
            peak[which, FIRST[stage] + j] = top

    lane = iota((block, 128), 1)

    def settle(which, stage, j, window):
        a = acc[which, FIRST[stage] + j, window]
        turned = pltpu.roll(a, 64, 1)
        mine = (iota(a.shape, 1) >= 64) if STAGES[stage][j][2] else (iota(a.shape, 1) < 64)
        sums = jnp.where(mine, a, turned)
        return a / sums, peak[which, FIRST[stage] + j, window] + jnp.log2(sums)

    def part_of(c):
        if c is None:
            return 0, slice(0, block), output_copies[0]
        return 1, slice(c * width, (c + 1) * width), output_copies[1 + c]

    def finish_partner(c=None):
        stage, window, copies = part_of(c)
        outs = [settle(1, stage, j, window) for j in range(len(STAGES[stage]))]
        count_rows = window.stop - window.start
        low_rows = iota((count_rows, 128), 1) < 64
        pair = jnp.where(low_rows, outs[0][0], outs[1][0]).astype(BF16)
        if stage == 0:
            obuf_a[0, 0:block] = pair
            out = outs[2][0]
            folded = jnp.where(low_half, pltpu.roll(out[half:], 64, 1), out[0:half])
            obuf_a[0, block:] = folded.astype(BF16)
        else:
            obuf_b[0, window] = pair
        copies[0].start()
        lane = iota((count_rows, 128), 1)
        sums = jnp.zeros((count_rows, 128), F32)
        for j, (_, lse) in enumerate(outs):
            sums = jnp.where(lane == j, lse, sums)
        if stage == 0:
            lse_a[0] = sums.T[0:8]
        else:
            lse_b[0, c] = sums.T[0:8]
        copies[1].start()

    def joined(c=None):
        stage, window, copies = part_of(c)
        own = [settle(0, stage, j, window) for j in range(len(STAGES[stage]))]
        for copy in copies:
            copy.wait_recv()
        sent = lse_a[1] if stage == 0 else lse_b[1, c]
        there = jnp.concatenate([sent, jnp.zeros((120, sent.shape[1]), F32)], axis=0).T
        outs = []
        for j, (out, lse) in enumerate(own):
            if stage == 1:
                out_there = obuf_b[1, window].astype(F32)
            elif j < 2:
                out_there = obuf_a[1, 0:block].astype(F32)
            else:
                folded = obuf_a[1, block:].astype(F32)
                out_there = jnp.concatenate([folded, pltpu.roll(folded, 64, 1)], axis=0)
            lse_there = there[:, j : j + 1]
            top = jnp.maximum(lse, lse_there)
            weight = jnp.exp2(lse - top)
            weight_there = jnp.exp2(lse_there - top)
            mixed = out * weight + out_there * weight_there
            outs.append(mixed / (weight + weight_there))
        return outs

    before = {
        1: lambda: ring_event(0, 2),
        4: lambda: ring_event(0, 3),
        5: lambda: (ring_wait(1, 2), ring_wait(1, 3)),
        6: lambda: (
            ring_event(0, 4),
            ring_forward(1, 2),
            ring_forward(1, 3),
            query_copies[0].wait_recv(),
            mask_queries(0, 1),
        ),
        9: lambda: ring_event(0, 5),
        10: lambda: (query_copies[1].wait_recv(), mask_queries(1, 1)),
        12: lambda: ring_event(0, 6),
        13: lambda: (finish_partner(), ring_event(1, 4)),
        15: lambda: ring_event(1, 5),
        17: lambda: ring_event(1, 6),
        18: lambda: [finish_partner(c) for c in range(rows)],
    }

    def step(i, carry):
        for k, actions in before.items():

            @pl.when(i == k)
            def _():
                actions()

        which = lookup(i, [s[1] for s in STEPS])
        slot = lookup(i, [s[2] for s in STEPS])
        kind = lookup(i, [2 * s[0] + s[3] - 1 for s in STEPS])
        for stage in range(2):
            for slots in (1, 2):
                pl.when(kind == 2 * stage + slots - 1)(
                    functools.partial(attend, stage, which, slot, slots)
                )
        return carry

    lax.fori_loop(0, len(STEPS), step, 0)


    load_ids.wait()
    load_table.wait()
    load_tqkv.wait()
    npos = table_v.shape[0]
    everything = frames * 16
    picked = jnp.where(iota((npos, frames), 0) == ids_v[...], 1.0, 0.0).astype(BF16)
    repeat = jnp.where(
        (iota((everything, frames), 0) >> 4) == iota((everything, frames), 1), 1.0, 0.0
    ).astype(BF16)
    onehot = dot_nt(repeat, picked).astype(BF16)
    position[...] = dot(onehot, table_v[...])
    other[...] = jnp.where(
        (iota((everything, everything), 0) & 15) == (iota((everything, everything), 1) & 15),
        0.0,
        -1e30,
    )
    twq[...] = jnp.zeros_like(twq)
    for part in range(3):
        twq[:, part * 384 : part * 384 + chans] = tqkv_v[:, part * chans : (part + 1) * chans]
    load_wout.wait()
    load_tout.wait()

    def wait_stat_send(k, carry):
        stat_copy(k).wait_send()
        return carry

    lax.fori_loop(1, n_patch, wait_stat_send, 0)

    @pl.when(me < n_patch - 1)
    def _():
        halo_copy(0).wait_send()

    @pl.when(me > 0)
    def _():
        halo_copy(1).wait_send()

    for stage in range(2):
        for i in range(7):
            for direction in range(2):
                ring_copy(stage, direction, i).wait_send()
        query_copies[stage].wait_send()
    store_fresh.wait()


    first = joined()
    pair = jnp.where(low, first[0], first[1]).astype(BF16)
    last = pltpu.roll(first[2], 64, 1)[:, 0:64].astype(BF16)
    hidden1[...] = (
        hidden1[...] + dot(pair, wout_v[0:128]) + dot(last, wout_v[256:chans])
    )
    quarter = frames // 4
    low_row = iota((width, 128), 1) < 64
    for c in range(rows):
        second = joined(c)
        window = slice(c * width, (c + 1) * width)
        pair = jnp.where(low_row, second[0], second[1]).astype(BF16)
        hid[window] = (hidden1[window] + dot(pair, wout_v[128:256])).astype(BF16)

        def send_out(k, carry, c=c):
            target = lax.rem(lax.div(frame, 4) + k, quarter) * 4 + c

            @pl.when(target != frame)
            def _():
                out_copy(target).start()

            return carry

        lax.fori_loop(0, quarter, send_out, 0)


    @pl.when(is_active(frame))
    def _():
        mine = group_rows(group_of(frame))
        keep = pltpu.make_async_copy(hid.at[mine], gathered.at[group_rows(frame)], own_sem.at[0])
        keep.start()
        keep.wait()

        def wait_out(k, carry):
            source = lax.rem(frame + k, frames)
            arrival(source, gathered, group_rows(source), out_recv).wait_recv()
            return carry

        lax.fori_loop(1, frames, wait_out, 0)

        inputs = gathered[...].astype(F32)
        norm2 = layer_norm(inputs + position[...]).astype(BF16)
        proj[:, 0:384] = (dot(norm2, twq[:, 0:384]) * (LOG2E / 8.0)).astype(BF16)
        proj[:, 384:] = dot(norm2, twq[:, 384:]).astype(BF16)

        low_t = iota((everything, 128), 1) < 64

        def lanes_of(h):
            return low_t if h % 2 == 0 else ~low_t

        def scores_t(h):
            tile = (h // 2) * 128
            q = proj[:, tile : tile + 128]
            q = jnp.where(lanes_of(h), q, jnp.zeros_like(q))
            return dot_nt(q, proj[:, 384 + tile : 384 + tile + 128])

        outs = []
        scores = scores_t(0)
        for h in range(HEADS):
            following = scores_t(h + 1) if h + 1 < HEADS else None
            tile = (h // 2) * 128
            v = proj[:, 768 + tile : 768 + tile + 128]
            v = jnp.where(lanes_of(h), v, jnp.ones_like(v))
            scores = scores + other[...]
            weights = jnp.exp2(scores - jnp.max(scores, axis=1, keepdims=True)).astype(BF16)
            mixed = dot(weights, v)
            outs.append(mixed / pltpu.roll(mixed, 64, 1))
            scores = following
        temporal = jnp.concatenate(
            [
                jnp.where(low_t, outs[0], outs[1]).astype(BF16),
                jnp.where(low_t, outs[2], outs[3]).astype(BF16),
                outs[4][:, 0:64].astype(BF16),
            ],
            axis=1,
        )
        done[...] = (inputs + dot(temporal, tout_v[...])).astype(BF16)

        def send_back(k, carry):
            back_copy(lax.rem(frame + k, frames)).start()
            return carry

        lax.fori_loop(1, frames, send_back, 0)
        put = pltpu.make_async_copy(done.at[group_rows(frame)], res_out.at[mine], own_sem.at[1])
        put.start()
        put.wait()

    for copies in output_copies:
        for copy in copies:
            copy.wait_send()

    def wait_out_send(k, carry):
        target = lax.rem(frame + k, frames)

        @pl.when(is_active(target))
        def _():
            out_copy(target).wait_send()

        return carry

    lax.fori_loop(1, frames, wait_out_send, 0)

    def wait_back(k, carry):
        source = lax.rem(frame + k, frames)

        @pl.when(is_active(source))
        def _():
            arrival(source, res_out, group_rows(group_of(source)), back_recv).wait_recv()

        return carry

    lax.fori_loop(1, frames, wait_back, 0)
    @pl.when(is_active(frame))
    def _():
        def wait_back_send(k, carry):
            back_copy(lax.rem(frame + k, frames)).wait_send()
            return carry

        lax.fori_loop(1, frames, wait_back_send, 0)


def emit_kernel(res_in, fresh_in, res_out, fresh_out, res_v, res_t, fresh_v, sems):
    rows, _, width = res_out.shape
    parts = [pl.ds(width * i, width) for i in range(rows)]

    def copies(k, src, dst):
        return pltpu.make_async_copy(src, dst, sems.at[k])

    res_loads = [copies(i, res_in.at[p], res_v.at[p]) for i, p in enumerate(parts)]
    fresh_loads = [copies(3 + i, fresh_in.at[p], fresh_v.at[p]) for i, p in enumerate(parts)]
    res_stores = [copies(6 + i, res_t.at[i], res_out.at[i]) for i in range(rows)]
    fresh_stores = [copies(9 + i, fresh_v.at[p], fresh_out.at[p]) for i, p in enumerate(parts)]
    for copy in res_loads + fresh_loads:
        copy.start()
    for i in range(rows):
        res_loads[i].wait()
        res_t[i] = res_v[parts[i]].astype(F32).T.astype(BF16)
        res_stores[i].start()
    for i in range(rows):
        fresh_loads[i].wait()
        fresh_stores[i].start()
    for copy in res_stores + fresh_stores:
        copy.wait()


def body(
    latents,
    stale_kv,
    frame_ids,
    timestep,
    conv_weight,
    time_proj,
    spatial_qkv,
    spatial_out,
    temporal_qkv,
    temporal_out,
    frame_table,
):
    rows, width, chans = latents.shape[1:]
    block = rows * width
    frames = frame_ids.shape[0]
    npos = frame_table.shape[0]
    dma = pltpu.SemaphoreType.DMA
    vmem = pltpu.VMEM
    anywhere = pl.BlockSpec(memory_space=pl.ANY)
    result, fresh = pl.pallas_call(
        functools.partial(kernel, rows, width, chans),
        out_shape=(
            jax.ShapeDtypeStruct((block, chans), BF16),
            jax.ShapeDtypeStruct((block, 2 * chans), BF16),
        ),
        in_specs=[anywhere, anywhere, pl.BlockSpec(memory_space=pltpu.SMEM)] + [anywhere] * 8,
        out_specs=(anywhere, anywhere),
        scratch_shapes=[
            vmem((rows, chans, width), BF16),
            vmem((block, 2 * chans), BF16),
            vmem((3, 3, chans, chans), BF16),
            vmem((chans, chans), BF16),
            vmem((chans, 3 * chans), BF16),
            vmem((chans, chans), BF16),
            vmem((1, frames), jnp.int32),
            vmem((npos, chans), BF16),
            vmem((chans, 3 * chans), BF16),
            vmem((chans, chans), BF16),
            vmem((block, chans), BF16),
            vmem((9, block, 384), BF16),
            vmem((9, block, 256), BF16),
            vmem((2, width, chans), BF16),
            vmem((block + 2 * width, chans), BF16),
            vmem((8, 128), F32),
            vmem((16, 8, 128), F32),
            vmem((block, chans), F32),
            vmem((chans, 384), BF16),
            vmem((block, 2 * chans), BF16),
            vmem((2, block + block // 2, 128), BF16),
            vmem((2, block, 128), BF16),
            vmem((2, HEADS, block, 128), BF16),
            vmem((2, HEADS, block, 128), F32),
            vmem((2, HEADS, block, 128), F32),
            vmem((2, block + block // 2, 128), BF16),
            vmem((2, block, 128), BF16),
            vmem((2, 8, block), F32),
            vmem((2, rows, 8, width), F32),
            vmem((block, chans), BF16),
            vmem((frames * 16, chans), F32),
            vmem((frames * 16, frames * 16), F32),
            vmem((chans, 3 * 384), BF16),
            vmem((frames * 16, chans), BF16),
            vmem((frames * 16, 3 * 384), BF16),
            vmem((frames * 16, chans), BF16),
            dma((10,)),
            dma((2,)),
            dma((2,)),
            dma((16,)),
            dma((16,)),
            dma((2, 2, 7)),
            dma((2, 2, 7)),
            dma((4 + 2 * rows,)),
            dma((4 + 2 * rows,)),
            dma((4,)),
            dma((frames,)),
            dma((frames,)),
            dma((frames,)),
            dma((frames,)),
        ],
        compiler_params=pltpu.CompilerParams(
            collective_id=0, has_side_effects=True, vmem_limit_bytes=60 * 1024 * 1024
        ),
        name="layer",
    )(
        jnp.transpose(latents, (0, 1, 3, 2)).reshape(rows, chans, width),
        stale_kv.reshape(block, 2 * chans),
        timestep,
        conv_weight,
        time_proj,
        spatial_qkv,
        spatial_out,
        frame_ids.reshape(1, frames),
        frame_table,
        temporal_qkv,
        temporal_out,
    )
    result, fresh = pl.pallas_call(
        emit_kernel,
        out_shape=(
            jax.ShapeDtypeStruct((rows, chans, width), BF16),
            jax.ShapeDtypeStruct(fresh.shape, BF16),
        ),
        in_specs=[anywhere] * 2,
        out_specs=(anywhere, anywhere),
        scratch_shapes=[
            vmem(result.shape, BF16),
            vmem((rows, chans, width), BF16),
            vmem(fresh.shape, BF16),
            dma((12,)),
        ],
        compiler_params=pltpu.CompilerParams(vmem_limit_bytes=62 * 1024 * 1024),
        name="emit",
    )(result, fresh)
    result = jnp.transpose(result.reshape(1, rows, chans, width), (0, 1, 3, 2))
    return result, fresh.reshape(stale_kv.shape)


def solution(mesh):
    return jax.shard_map(
        body,
        mesh=mesh,
        in_specs=(
            P("frame", "patch", None, None),
            P("frame", "patch", None, None),
            P(),
            P(),
            P(),
            P(),
            P(),
            P(),
            P(),
            P(),
            P(),
        ),
        out_specs=(P("frame", "patch", None, None), P("frame", "patch", None, None)),
        check_vma=False,
    )
```

```python
import functools
import math

import jax
import jax.numpy as jnp
from jax import lax
from jax.experimental import pallas as pl
from jax.experimental.pallas import tpu as pltpu
from jax.sharding import PartitionSpec as P

HEADS = 5
GROUPS = 32
F32 = jnp.float32
BF16 = jnp.bfloat16
MESH = pl.DeviceIdType.MESH
LOG2E = math.log2(math.e)
HIGHEST = lax.Precision.HIGHEST

STAGES = (((1, 2, True), (1, 2, False), (0, 0, False)), ((0, 1, True), (0, 1, False)))
FIRST = (0, 3)
FRESH = 8
STEPS = (
    (0, 0, FRESH, 1),
    (1, 0, FRESH, 1),
    (0, 0, 1, 2),
    (1, 0, 1, 2),
    (0, 0, 3, 2),
    (1, 0, 3, 2),
    (0, 1, 0, 1),
    (0, 1, 1, 2),
    (0, 1, 3, 2),
    (0, 1, 5, 2),
    (1, 1, 0, 1),
    (1, 1, 1, 2),
    (0, 1, 7, 1),
    (1, 1, 3, 2),
    (0, 0, 5, 2),
    (1, 1, 5, 2),
    (0, 0, 7, 1),
    (1, 1, 7, 1),
    (1, 0, 5, 2),
    (1, 0, 7, 1),
)


def iota(shape, dim):
    return lax.broadcasted_iota(jnp.int32, shape, dim)


def dot(a, b, precision=None):
    return lax.dot_general(
        a, b, (((1,), (0,)), ((), ())), preferred_element_type=F32, precision=precision
    )


def dot_nt(a, b, precision=None):
    return lax.dot_general(
        a, b, (((1,), (1,)), ((), ())), preferred_element_type=F32, precision=precision
    )


def layer_norm(values):
    centre = values - jnp.mean(values, axis=-1, keepdims=True)
    spread = jnp.mean(centre * centre, axis=-1, keepdims=True)
    return centre * lax.rsqrt(spread + 1e-05)


def group_of_channel(chans):
    per_group = chans // GROUPS
    chan = iota((chans, 128), 0)
    group = iota((chans, 128), 1)
    inside = (chan >= group * per_group) & (chan < (group + 1) * per_group)
    return jnp.where(inside, 1.0, 0.0).astype(F32)


def from_step(i, k):
    return lax.div(i - k + 32, 32)


def lookup(i, values):
    out = values[0]
    for k in range(1, len(values)):
        if values[k] != values[k - 1]:
            out = out + (values[k] - values[k - 1]) * from_step(i, k)
    return out


def kernel(
    rows,
    width,
    chans,
    lat_in,
    stale_in,
    time_ref,
    conv_in,
    tproj_in,
    qkv_in,
    wout_in,
    ids_in,
    table_in,
    tqkv_in,
    tout_in,
    res_out,
    fresh_out,
    lat_t,
    stale_v,
    conv_w,
    tproj_v,
    qkv_v,
    wout_v,
    ids_v,
    table_v,
    tqkv_v,
    tout_v,
    lat,
    kv_a,
    kv_b,
    halo,
    act,
    stat_out,
    stat_in,
    hidden1,
    wq,
    fresh_v,
    qbuf_a,
    qbuf_b,
    qmask,
    peak,
    acc,
    obuf_a,
    obuf_b,
    lse_a,
    lse_b,
    hid,
    position,
    other,
    twq,
    gathered,
    proj,
    done,
    load_sem,
    halo_send,
    halo_recv,
    stat_send,
    stat_recv,
    ring_send,
    ring_recv,
    part_send,
    part_recv,
    own_sem,
    out_send,
    out_recv,
    back_send,
    back_recv,
):
    block = rows * width
    half = block // 2
    me = lax.axis_index("patch")
    n_patch = lax.axis_size("patch")
    ring = n_patch // 2
    z = lax.rem(me, ring)
    base_z = me - z
    right = base_z + lax.rem(z + 1, ring)
    left = base_z + lax.rem(z + ring - 1, ring)
    partner = lax.rem(me + ring, n_patch)
    frame = lax.axis_index("frame")
    frames = lax.axis_size("frame")
    kv = (kv_a, kv_b)
    qbuf = (qbuf_a, qbuf_b)


    loads = [
        pltpu.make_async_copy(src, dst, load_sem.at[i])
        for i, (src, dst) in enumerate(
            (
                (stale_in, stale_v),
                (lat_in, lat_t),
                (tproj_in, tproj_v),
                (conv_in, conv_w),
                (qkv_in, qkv_v),
                (wout_in, wout_v),
                (ids_in, ids_v),
                (table_in, table_v),
                (tqkv_in, tqkv_v),
                (tout_in, tout_v),
            )
        )
    ]
    (
        load_stale,
        load_lat,
        load_tproj,
        load_conv,
        load_qkv,
        load_wout,
        load_ids,
        load_table,
        load_tqkv,
        load_tout,
    ) = loads

    def ring_copy(stage, direction, i):
        dist = i // 2 + 1
        part = i % 2 if direction == 0 else 1 - i % 2
        window = pl.ds(part * half, half)
        dst_slot = 7 if dist == 4 else 2 * dist - 1 + direction
        src_slot = 0 if dist == 1 else 2 * dist - 3 + direction
        return pltpu.make_async_remote_copy(
            src_ref=kv[stage].at[src_slot, window],
            dst_ref=kv[stage].at[dst_slot, window],
            send_sem=ring_send.at[stage, direction, i],
            recv_sem=ring_recv.at[stage, direction, i],
            device_id={"patch": right if direction == 0 else left},
            device_id_type=MESH,
        )

    def ring_start(stage):
        for i in range(2):
            for direction in range(2):
                ring_copy(stage, direction, i).start()

    def ring_wait(stage, e):
        for direction in range(2):
            ring_copy(stage, direction, e).wait_recv()

    def ring_forward(stage, e):
        for direction in range(2):
            ring_copy(stage, direction, e + 2).start()

    def ring_event(stage, e):
        for direction in range(2):
            ring_copy(stage, direction, e).wait_recv()
            if e + 2 < 7:
                ring_copy(stage, direction, e + 2).start()

    def halo_copy(direction):
        return pltpu.make_async_remote_copy(
            src_ref=lat_t.at[rows - 1 if direction == 0 else 0],
            dst_ref=halo.at[direction],
            send_sem=halo_send.at[direction],
            recv_sem=halo_recv.at[direction],
            device_id={"patch": me + 1 if direction == 0 else me - 1},
            device_id_type=MESH,
        )

    def stat_copy(k):
        return pltpu.make_async_remote_copy(
            src_ref=stat_out,
            dst_ref=stat_in.at[k],
            send_sem=stat_send.at[k],
            recv_sem=stat_recv.at[k],
            device_id={"patch": lax.rem(me + k, n_patch)},
            device_id_type=MESH,
        )

    def part_copy(src, dst, k):
        return pltpu.make_async_remote_copy(
            src_ref=src,
            dst_ref=dst,
            send_sem=part_send.at[k],
            recv_sem=part_recv.at[k],
            device_id={"patch": partner},
            device_id_type=MESH,
        )

    query_copies = [part_copy(qbuf[s].at[0], qbuf[s].at[1], s) for s in range(2)]
    output_copies = [(part_copy(obuf_a.at[0], obuf_a.at[1], 2), part_copy(lse_a.at[0], lse_a.at[1], 3))]
    for c in range(rows):
        window = pl.ds(c * width, width)
        output_copies.append(
            (
                part_copy(obuf_b.at[0, window], obuf_b.at[1, window], 4 + 2 * c),
                part_copy(lse_b.at[0, c], lse_b.at[1, c], 5 + 2 * c),
            )
        )

    def group_rows(g):
        return pl.ds(pl.multiple_of(g * 16, 16), 16)

    per_row = width // 16

    def is_active(f):
        return lax.rem(f, 4) < rows

    def group_of(f):
        return lax.rem(f, 4) * per_row + lax.div(f, 4)

    def out_copy(target):
        return pltpu.make_async_remote_copy(
            src_ref=hid.at[group_rows(group_of(target))],
            dst_ref=gathered.at[group_rows(frame)],
            send_sem=out_send.at[target],
            recv_sem=out_recv.at[frame],
            device_id={"frame": target},
            device_id_type=MESH,
        )

    def back_copy(target):
        return pltpu.make_async_remote_copy(
            src_ref=done.at[group_rows(target)],
            dst_ref=res_out.at[group_rows(group_of(frame))],
            send_sem=back_send.at[target],
            recv_sem=back_recv.at[frame],
            device_id={"frame": target},
            device_id_type=MESH,
        )

    def arrival(source, buffer, rows_of_it, sems):
        return pltpu.make_async_remote_copy(
            src_ref=done.at[pl.ds(0, 16)],
            dst_ref=buffer.at[rows_of_it],
            send_sem=out_send.at[0],
            recv_sem=sems.at[source],
            device_id={"frame": source},
            device_id_type=MESH,
        )


    barrier = pltpu.get_barrier_semaphore()

    def greet_patch(k, carry):
        pl.semaphore_signal(
            barrier,
            inc=1,
            device_id={"patch": lax.rem(me + k, n_patch)},
            device_id_type=MESH,
        )
        return carry

    def greet_frame(k, carry):
        pl.semaphore_signal(
            barrier,
            inc=1,
            device_id={"frame": lax.rem(frame + k, frames)},
            device_id_type=MESH,
        )
        return carry

    lax.fori_loop(1, n_patch, greet_patch, 0)
    lax.fori_loop(1, frames, greet_frame, 0)
    for load in loads:
        load.start()

    low = iota((block, 128), 1) < 64

    def arrange(source, slot):
        kv_a[slot, :, 0:128] = jnp.where(low, source[:, 256:384], source[:, 512:640])
        kv_a[slot, :, 128:256] = source[:, 0:128]
        kv_a[slot, :, 256:384] = source[:, 320:448]
        kv_b[slot, :, 0:128] = source[:, 128:256]
        kv_b[slot, :, 128:256] = source[:, 448:576]

    load_stale.wait()
    arrange(stale_v, 0)
    load_lat.wait()
    for r in range(rows):
        lat[r * width : (r + 1) * width] = lat_t[r].astype(F32).T.astype(BF16)

    pl.semaphore_wait(barrier, n_patch - 1 + frames - 1)
    @pl.when(me < n_patch - 1)
    def _():
        halo_copy(0).start()

    @pl.when(me > 0)
    def _():
        halo_copy(1).start()

    ring_start(0)

    values = lat[...].astype(F32)
    col_sum = jnp.sum(values, axis=0, keepdims=True)
    col_sq = jnp.sum(values * values, axis=0, keepdims=True)
    row8 = iota((8, chans), 0)
    cols = jnp.where(row8 == 0, col_sum, jnp.where(row8 == 1, col_sq, 0.0))
    member = group_of_channel(chans)
    stat_out[...] = dot(cols, member, HIGHEST)

    def send_stat(k, carry):
        stat_copy(k).start()
        return carry

    lax.fori_loop(1, n_patch, send_stat, 0)
    ring_start(1)

    load_tproj.wait()
    lane_c = iota((8, chans), 1)
    half_c = chans // 2
    order = jnp.where(lane_c < half_c, lane_c, lane_c - half_c).astype(F32)
    freqs = jnp.exp(-math.log(10000.0) * order / half_c)
    angles = time_ref[0].astype(F32) * freqs
    emb = jnp.where(lane_c < half_c, jnp.cos(angles), jnp.sin(angles)).astype(BF16)
    bias = dot(emb, tproj_v[...])[0:1]
    load_conv.wait()
    load_qkv.wait()
    wq[...] = jnp.zeros_like(wq)
    wq[:, 0:chans] = qkv_v[:, 0:chans]
    peak[...] = jnp.full(peak.shape, -1e30, F32)
    acc[...] = jnp.zeros(acc.shape, F32)


    def wait_stat(k, carry):
        stat_copy(k).wait_recv()
        return carry

    lax.fori_loop(1, n_patch, wait_stat, 0)
    total = stat_out[...]
    for k in range(1, 16):
        total = total + stat_in[k]
    count = block * (chans // GROUPS) * n_patch
    mean = total[0:1] / count
    var = total[1:2] / count - mean * mean
    rstd = lax.rsqrt(var + 1e-05)
    row8g = iota((8, 128), 0)
    spread = dot_nt(jnp.where(row8g == 0, mean, jnp.where(row8g == 1, rstd, 0.0)), member, HIGHEST)
    mean_c, rstd_c = spread[0:1], spread[1:2]

    def activate(x):
        normed = (x.astype(F32) - mean_c) * rstd_c
        return (normed / (1.0 + jnp.exp(-normed))).astype(BF16)

    act[width : width + block] = activate(lat[...])

    @pl.when(me > 0)
    def _():
        halo_copy(0).wait_recv()
        act[0:width] = activate(halo[0].astype(F32).T)

    @pl.when(me == 0)
    def _():
        act[0:width] = jnp.zeros((width, chans), BF16)

    @pl.when(me < n_patch - 1)
    def _():
        halo_copy(1).wait_recv()
        act[width + block :] = activate(halo[1].astype(F32).T)

    @pl.when(me == n_patch - 1)
    def _():
        act[width + block :] = jnp.zeros((width, chans), BF16)

    ring_event(0, 0)


    column = iota((block, chans), 0) & (width - 1)

    def conv_column(step):
        out = dot(act[0:block], conv_w[0, step])
        out = out + dot(act[width : width + block], conv_w[1, step])
        return out + dot(act[2 * width : 2 * width + block], conv_w[2, step])

    conv = conv_column(1)
    conv = conv + jnp.where(column == 0, 0.0, pltpu.roll(conv_column(0), 1, 0))
    ring_event(0, 1)
    conv = conv + jnp.where(column == width - 1, 0.0, pltpu.roll(conv_column(2), block - 1, 0))
    h1 = lat[...].astype(F32) + conv + bias
    hidden1[...] = h1
    norm1 = layer_norm(h1).astype(BF16)
    queries = dot(norm1, wq[...]) * (LOG2E / 8.0)
    low_half = iota((half, 128), 1) < 64
    qbuf_a[0, 0:block] = queries[:, 0:128].astype(BF16)
    folded = jnp.where(
        low_half, queries[0:half, 256:384], pltpu.roll(queries[half:, 256:384], 64, 1)
    )
    qbuf_a[0, block:] = folded.astype(BF16)
    query_copies[0].start()
    qbuf_b[0] = queries[:, 128:256].astype(BF16)
    query_copies[1].start()
    ring_event(1, 0)
    ring_event(1, 1)
    fresh_v[...] = dot(norm1, qkv_v[:, chans:]).astype(BF16)
    store_fresh = pltpu.make_async_copy(fresh_v, fresh_out, own_sem.at[2])
    store_fresh.start()
    arrange(fresh_v, FRESH)

    def mask_queries(stage, which):
        def keep(tile, lanes):
            return jnp.where(lanes, tile, jnp.zeros_like(tile))

        if stage == 0:
            tile = qbuf_a[which, 0:block]
            qmask[which, 0] = keep(tile, low)
            qmask[which, 1] = keep(tile, ~low)
            tile = qbuf_a[which, block:].astype(F32)
            qmask[which, 2, 0:half] = jnp.where(low_half, tile, 0.0).astype(BF16)
            tile = pltpu.roll(tile, 64, 1)
            qmask[which, 2, half:] = jnp.where(low_half, tile, 0.0).astype(BF16)
        else:
            tile = qbuf_b[which]
            qmask[which, 3] = keep(tile, low)
            qmask[which, 4] = keep(tile, ~low)

    mask_queries(0, 0)
    mask_queries(1, 0)


    def attend(stage, which, slot, slots):
        heads = STAGES[stage]
        keys = slots * block
        low_keys = iota((keys, 128), 1) < 64

        def tile_of(t):
            return kv[stage][pl.ds(slot, slots), :, t * 128 : t * 128 + 128].reshape(keys, 128)

        def scores_of(j):
            return dot_nt(qmask[which, FIRST[stage] + j], tile_of(heads[j][0]))

        accs = [acc[which, FIRST[stage] + j] for j in range(len(heads))]
        peaks = [peak[which, FIRST[stage] + j] for j in range(len(heads))]
        scores = scores_of(0)
        results = []
        for j, (_, vt, in_low) in enumerate(heads):
            following = scores_of(j + 1) if j + 1 < len(heads) else None
            top = jnp.maximum(peaks[j], jnp.max(scores, axis=1, keepdims=True))
            weights = jnp.exp2(scores - jnp.concatenate([top] * (keys // 128), axis=1))
            vals = tile_of(vt)
            vals = jnp.where(low_keys if in_low else ~low_keys, vals, jnp.ones_like(vals))
            scale = jnp.exp2(peaks[j] - top)
            results.append((accs[j] * scale + dot(weights.astype(BF16), vals), top))
            scores = following
        for j, (new_acc, top) in enumerate(results):
            acc[which, FIRST[stage] + j] = new_acc
            peak[which, FIRST[stage] + j] = top

    lane = iota((block, 128), 1)

    def settle(which, stage, j, window):
        a = acc[which, FIRST[stage] + j, window]
        turned = pltpu.roll(a, 64, 1)
        mine = (iota(a.shape, 1) >= 64) if STAGES[stage][j][2] else (iota(a.shape, 1) < 64)
        sums = jnp.where(mine, a, turned)
        return a / sums, peak[which, FIRST[stage] + j, window] + jnp.log2(sums)

    def part_of(c):
        if c is None:
            return 0, slice(0, block), output_copies[0]
        return 1, slice(c * width, (c + 1) * width), output_copies[1 + c]

    def finish_partner(c=None):
        stage, window, copies = part_of(c)
        outs = [settle(1, stage, j, window) for j in range(len(STAGES[stage]))]
        count_rows = window.stop - window.start
        low_rows = iota((count_rows, 128), 1) < 64
        pair = jnp.where(low_rows, outs[0][0], outs[1][0]).astype(BF16)
        if stage == 0:
            obuf_a[0, 0:block] = pair
            out = outs[2][0]
            folded = jnp.where(low_half, pltpu.roll(out[half:], 64, 1), out[0:half])
            obuf_a[0, block:] = folded.astype(BF16)
        else:
            obuf_b[0, window] = pair
        copies[0].start()
        lane = iota((count_rows, 128), 1)
        sums = jnp.zeros((count_rows, 128), F32)
        for j, (_, lse) in enumerate(outs):
            sums = jnp.where(lane == j, lse, sums)
        if stage == 0:
            lse_a[0] = sums.T[0:8]
        else:
            lse_b[0, c] = sums.T[0:8]
        copies[1].start()

    def joined(c=None):
        stage, window, copies = part_of(c)
        own = [settle(0, stage, j, window) for j in range(len(STAGES[stage]))]
        for copy in copies:
            copy.wait_recv()
        sent = lse_a[1] if stage == 0 else lse_b[1, c]
        there = jnp.concatenate([sent, jnp.zeros((120, sent.shape[1]), F32)], axis=0).T
        outs = []
        for j, (out, lse) in enumerate(own):
            if stage == 1:
                out_there = obuf_b[1, window].astype(F32)
            elif j < 2:
                out_there = obuf_a[1, 0:block].astype(F32)
            else:
                folded = obuf_a[1, block:].astype(F32)
                out_there = jnp.concatenate([folded, pltpu.roll(folded, 64, 1)], axis=0)
            lse_there = there[:, j : j + 1]
            top = jnp.maximum(lse, lse_there)
            weight = jnp.exp2(lse - top)
            weight_there = jnp.exp2(lse_there - top)
            mixed = out * weight + out_there * weight_there
            outs.append(mixed / (weight + weight_there))
        return outs

    everything = frames * 16

    def prepare_temporal():
        load_ids.wait()
        load_table.wait()
        load_tqkv.wait()
        npos = table_v.shape[0]
        picked = jnp.where(iota((npos, frames), 0) == ids_v[...], 1.0, 0.0).astype(BF16)
        repeat = jnp.where(
            (iota((everything, frames), 0) >> 4) == iota((everything, frames), 1), 1.0, 0.0
        ).astype(BF16)
        onehot = dot_nt(repeat, picked).astype(BF16)
        position[...] = dot(onehot, table_v[...])
        other[...] = jnp.where(
            (iota((everything, everything), 0) & 15) == (iota((everything, everything), 1) & 15),
            0.0,
            -1e30,
        )
        twq[...] = jnp.zeros_like(twq)
        for part in range(3):
            twq[:, part * 384 : part * 384 + chans] = tqkv_v[:, part * chans : (part + 1) * chans]

    before = {
        1: lambda: ring_event(0, 2),
        4: lambda: ring_event(0, 3),
        5: lambda: (ring_wait(1, 2), ring_wait(1, 3)),
        6: lambda: (
            prepare_temporal(),
            ring_event(0, 4),
            ring_forward(1, 2),
            ring_forward(1, 3),
            query_copies[0].wait_recv(),
            mask_queries(0, 1),
        ),
        9: lambda: ring_event(0, 5),
        10: lambda: (query_copies[1].wait_recv(), mask_queries(1, 1)),
        12: lambda: ring_event(0, 6),
        13: lambda: (finish_partner(), ring_event(1, 4)),
        15: lambda: ring_event(1, 5),
        17: lambda: ring_event(1, 6),
        18: lambda: [finish_partner(c) for c in range(rows)],
    }

    def step(i, carry):
        for k, actions in before.items():

            @pl.when(i == k)
            def _():
                actions()

        which = lookup(i, [s[1] for s in STEPS])
        slot = lookup(i, [s[2] for s in STEPS])
        kind = lookup(i, [2 * s[0] + s[3] - 1 for s in STEPS])
        for stage in range(2):
            for slots in (1, 2):
                pl.when(kind == 2 * stage + slots - 1)(
                    functools.partial(attend, stage, which, slot, slots)
                )
        return carry

    lax.fori_loop(0, len(STEPS), step, 0)

    load_wout.wait()
    load_tout.wait()

    def wait_stat_send(k, carry):
        stat_copy(k).wait_send()
        return carry

    lax.fori_loop(1, n_patch, wait_stat_send, 0)

    @pl.when(me < n_patch - 1)
    def _():
        halo_copy(0).wait_send()

    @pl.when(me > 0)
    def _():
        halo_copy(1).wait_send()

    for stage in range(2):
        for i in range(7):
            for direction in range(2):
                ring_copy(stage, direction, i).wait_send()
        query_copies[stage].wait_send()
    store_fresh.wait()


    first = joined()
    pair = jnp.where(low, first[0], first[1]).astype(BF16)
    last = pltpu.roll(first[2], 64, 1)[:, 0:64].astype(BF16)
    hidden1[...] = (
        hidden1[...] + dot(pair, wout_v[0:128]) + dot(last, wout_v[256:chans])
    )
    quarter = frames // 4
    low_row = iota((width, 128), 1) < 64
    for c in range(rows):
        second = joined(c)
        window = slice(c * width, (c + 1) * width)
        pair = jnp.where(low_row, second[0], second[1]).astype(BF16)
        hid[window] = (hidden1[window] + dot(pair, wout_v[128:256])).astype(BF16)

        def send_out(k, carry, c=c):
            target = lax.rem(lax.div(frame, 4) + k, quarter) * 4 + c

            @pl.when(target != frame)
            def _():
                out_copy(target).start()

            return carry

        lax.fori_loop(0, quarter, send_out, 0)


    @pl.when(is_active(frame))
    def _():
        mine = group_rows(group_of(frame))
        keep = pltpu.make_async_copy(hid.at[mine], gathered.at[group_rows(frame)], own_sem.at[0])
        keep.start()
        keep.wait()

        def wait_out(k, carry):
            source = lax.rem(frame + k, frames)
            arrival(source, gathered, group_rows(source), out_recv).wait_recv()
            return carry

        lax.fori_loop(1, frames, wait_out, 0)

        inputs = gathered[...].astype(F32)
        norm2 = layer_norm(inputs + position[...]).astype(BF16)
        proj[:, 0:384] = (dot(norm2, twq[:, 0:384]) * (LOG2E / 8.0)).astype(BF16)
        proj[:, 384:] = dot(norm2, twq[:, 384:]).astype(BF16)

        low_t = iota((everything, 128), 1) < 64
        upper = everything // 2

        def lanes_of(h):
            return low_t if h % 2 == 0 else ~low_t

        def masked(h, rows_of_it, first_lane, fill):
            tile = proj[rows_of_it, first_lane + (h // 2) * 128 : first_lane + (h // 2) * 128 + 128]
            return jnp.where(lanes_of(h)[0 : tile.shape[0]], tile, fill(tile))

        def send_half(part):
            window = slice(part * upper, (part + 1) * upper)

            def scores_t(h):
                keys = proj[:, 384 + (h // 2) * 128 : 384 + (h // 2) * 128 + 128]
                return dot_nt(masked(h, window, 0, jnp.zeros_like), keys)

            low_h = low_t[0:upper]
            outs = []
            scores = scores_t(0)
            for h in range(HEADS):
                following = scores_t(h + 1) if h + 1 < HEADS else None
                scores = scores + other[window]
                weights = jnp.exp2(scores - jnp.max(scores, axis=1, keepdims=True)).astype(BF16)
                mixed = dot(weights, masked(h, slice(0, everything), 768, jnp.ones_like))
                outs.append(mixed / pltpu.roll(mixed, 64, 1))
                scores = following
            temporal = jnp.concatenate(
                [
                    jnp.where(low_h, outs[0], outs[1]).astype(BF16),
                    jnp.where(low_h, outs[2], outs[3]).astype(BF16),
                    outs[4][:, 0:64].astype(BF16),
                ],
                axis=1,
            )
            done[window] = (
                gathered[window].astype(F32) + dot(temporal, tout_v[...])
            ).astype(BF16)

            def send_back(k, carry):
                target = part * (frames // 2) + lax.rem(frame + k, frames // 2)

                @pl.when(target != frame)
                def _():
                    back_copy(target).start()

                return carry

            lax.fori_loop(0, frames // 2, send_back, 0)

        send_half(0)
        send_half(1)
        put = pltpu.make_async_copy(done.at[group_rows(frame)], res_out.at[mine], own_sem.at[1])
        put.start()
        put.wait()

    for copies in output_copies:
        for copy in copies:
            copy.wait_send()

    def wait_out_send(k, carry):
        target = lax.rem(frame + k, frames)

        @pl.when(is_active(target))
        def _():
            out_copy(target).wait_send()

        return carry

    lax.fori_loop(1, frames, wait_out_send, 0)

    def wait_back(k, carry):
        source = lax.rem(frame + k, frames)

        @pl.when(is_active(source))
        def _():
            arrival(source, res_out, group_rows(group_of(source)), back_recv).wait_recv()

        return carry

    lax.fori_loop(1, frames, wait_back, 0)
    @pl.when(is_active(frame))
    def _():
        def wait_back_send(k, carry):
            back_copy(lax.rem(frame + k, frames)).wait_send()
            return carry

        lax.fori_loop(1, frames, wait_back_send, 0)


def emit_kernel(res_in, fresh_in, res_out, fresh_out, res_v, res_t, fresh_v, sems):
    rows, _, width = res_out.shape
    parts = [pl.ds(width * i, width) for i in range(rows)]

    def copies(k, src, dst):
        return pltpu.make_async_copy(src, dst, sems.at[k])

    res_loads = [copies(i, res_in.at[p], res_v.at[p]) for i, p in enumerate(parts)]
    fresh_loads = [copies(3 + i, fresh_in.at[p], fresh_v.at[p]) for i, p in enumerate(parts)]
    res_stores = [copies(6 + i, res_t.at[i], res_out.at[i]) for i in range(rows)]
    fresh_stores = [copies(9 + i, fresh_v.at[p], fresh_out.at[p]) for i, p in enumerate(parts)]
    for copy in res_loads + fresh_loads:
        copy.start()
    for i in range(rows):
        res_loads[i].wait()
        res_t[i] = res_v[parts[i]].astype(F32).T.astype(BF16)
        res_stores[i].start()
    for i in range(rows):
        fresh_loads[i].wait()
        fresh_stores[i].start()
    for copy in res_stores + fresh_stores:
        copy.wait()


def body(
    latents,
    stale_kv,
    frame_ids,
    timestep,
    conv_weight,
    time_proj,
    spatial_qkv,
    spatial_out,
    temporal_qkv,
    temporal_out,
    frame_table,
):
    rows, width, chans = latents.shape[1:]
    block = rows * width
    frames = frame_ids.shape[0]
    npos = frame_table.shape[0]
    dma = pltpu.SemaphoreType.DMA
    vmem = pltpu.VMEM
    anywhere = pl.BlockSpec(memory_space=pl.ANY)
    result, fresh = pl.pallas_call(
        functools.partial(kernel, rows, width, chans),
        out_shape=(
            jax.ShapeDtypeStruct((block, chans), BF16),
            jax.ShapeDtypeStruct((block, 2 * chans), BF16),
        ),
        in_specs=[anywhere, anywhere, pl.BlockSpec(memory_space=pltpu.SMEM)] + [anywhere] * 8,
        out_specs=(anywhere, anywhere),
        scratch_shapes=[
            vmem((rows, chans, width), BF16),
            vmem((block, 2 * chans), BF16),
            vmem((3, 3, chans, chans), BF16),
            vmem((chans, chans), BF16),
            vmem((chans, 3 * chans), BF16),
            vmem((chans, chans), BF16),
            vmem((1, frames), jnp.int32),
            vmem((npos, chans), BF16),
            vmem((chans, 3 * chans), BF16),
            vmem((chans, chans), BF16),
            vmem((block, chans), BF16),
            vmem((9, block, 384), BF16),
            vmem((9, block, 256), BF16),
            vmem((2, chans, width), BF16),
            vmem((block + 2 * width, chans), BF16),
            vmem((8, 128), F32),
            vmem((16, 8, 128), F32),
            vmem((block, chans), F32),
            vmem((chans, 384), BF16),
            vmem((block, 2 * chans), BF16),
            vmem((2, block + block // 2, 128), BF16),
            vmem((2, block, 128), BF16),
            vmem((2, HEADS, block, 128), BF16),
            vmem((2, HEADS, block, 128), F32),
            vmem((2, HEADS, block, 128), F32),
            vmem((2, block + block // 2, 128), BF16),
            vmem((2, block, 128), BF16),
            vmem((2, 8, block), F32),
            vmem((2, rows, 8, width), F32),
            vmem((block, chans), BF16),
            vmem((frames * 16, chans), F32),
            vmem((frames * 16, frames * 16), F32),
            vmem((chans, 3 * 384), BF16),
            vmem((frames * 16, chans), BF16),
            vmem((frames * 16, 3 * 384), BF16),
            vmem((frames * 16, chans), BF16),
            dma((10,)),
            dma((2,)),
            dma((2,)),
            dma((16,)),
            dma((16,)),
            dma((2, 2, 7)),
            dma((2, 2, 7)),
            dma((4 + 2 * rows,)),
            dma((4 + 2 * rows,)),
            dma((4,)),
            dma((frames,)),
            dma((frames,)),
            dma((frames,)),
            dma((frames,)),
        ],
        compiler_params=pltpu.CompilerParams(
            collective_id=0, has_side_effects=True, vmem_limit_bytes=60 * 1024 * 1024
        ),
        name="layer",
    )(
        jnp.transpose(latents, (0, 1, 3, 2)).reshape(rows, chans, width),
        stale_kv.reshape(block, 2 * chans),
        timestep,
        conv_weight,
        time_proj,
        spatial_qkv,
        spatial_out,
        frame_ids.reshape(1, frames),
        frame_table,
        temporal_qkv,
        temporal_out,
    )
    result, fresh = pl.pallas_call(
        emit_kernel,
        out_shape=(
            jax.ShapeDtypeStruct((rows, chans, width), BF16),
            jax.ShapeDtypeStruct(fresh.shape, BF16),
        ),
        in_specs=[anywhere] * 2,
        out_specs=(anywhere, anywhere),
        scratch_shapes=[
            vmem(result.shape, BF16),
            vmem((rows, chans, width), BF16),
            vmem(fresh.shape, BF16),
            dma((12,)),
        ],
        compiler_params=pltpu.CompilerParams(vmem_limit_bytes=62 * 1024 * 1024),
        name="emit",
    )(result, fresh)
    result = jnp.transpose(result.reshape(1, rows, chans, width), (0, 1, 3, 2))
    return result, fresh.reshape(stale_kv.shape)


def solution(mesh):
    return jax.shard_map(
        body,
        mesh=mesh,
        in_specs=(
            P("frame", "patch", None, None),
            P("frame", "patch", None, None),
            P(),
            P(),
            P(),
            P(),
            P(),
            P(),
            P(),
            P(),
            P(),
        ),
        out_specs=(P("frame", "patch", None, None), P("frame", "patch", None, None)),
        check_vma=False,
    )
```

```python
import functools
import math

import jax
import jax.numpy as jnp
from jax import lax
from jax.experimental import pallas as pl
from jax.experimental.pallas import tpu as pltpu
from jax.sharding import PartitionSpec as P

HEADS = 5
GROUPS = 32
F32 = jnp.float32
BF16 = jnp.bfloat16
MESH = pl.DeviceIdType.MESH
LOG2E = math.log2(math.e)
HIGHEST = lax.Precision.HIGHEST

STAGES = (((1, 2, True), (1, 2, False), (0, 0, False)), ((0, 1, True), (0, 1, False)))
FIRST = (0, 3)
FRESH = 8
STEPS = (
    (0, 0, FRESH, 1),
    (1, 0, FRESH, 1),
    (0, 0, 1, 2),
    (1, 0, 1, 2),
    (0, 0, 3, 2),
    (1, 0, 3, 2),
    (0, 1, 0, 1),
    (0, 1, 1, 2),
    (0, 1, 3, 2),
    (0, 1, 5, 2),
    (1, 1, 0, 1),
    (1, 1, 1, 2),
    (0, 1, 7, 1),
    (1, 1, 3, 2),
    (0, 0, 5, 2),
    (1, 1, 5, 2),
    (0, 0, 7, 1),
    (1, 1, 7, 1),
    (1, 0, 5, 2),
    (1, 0, 7, 1),
)


def iota(shape, dim):
    return lax.broadcasted_iota(jnp.int32, shape, dim)


def dot(a, b, precision=None):
    return lax.dot_general(
        a, b, (((1,), (0,)), ((), ())), preferred_element_type=F32, precision=precision
    )


def dot_nt(a, b, precision=None):
    return lax.dot_general(
        a, b, (((1,), (1,)), ((), ())), preferred_element_type=F32, precision=precision
    )


def layer_norm(values):
    centre = values - jnp.mean(values, axis=-1, keepdims=True)
    spread = jnp.mean(centre * centre, axis=-1, keepdims=True)
    return centre * lax.rsqrt(spread + 1e-05)


def group_of_channel(chans):
    per_group = chans // GROUPS
    chan = iota((chans, 128), 0)
    group = iota((chans, 128), 1)
    inside = (chan >= group * per_group) & (chan < (group + 1) * per_group)
    return jnp.where(inside, 1.0, 0.0).astype(F32)


def from_step(i, k):
    return lax.div(i - k + 32, 32)


def lookup(i, values):
    out = values[0]
    for k in range(1, len(values)):
        if values[k] != values[k - 1]:
            out = out + (values[k] - values[k - 1]) * from_step(i, k)
    return out


def kernel(
    rows,
    width,
    chans,
    lat_in,
    stale_in,
    time_ref,
    conv_in,
    tproj_in,
    qkv_in,
    wout_in,
    ids_in,
    table_in,
    tqkv_in,
    tout_in,
    res_out,
    fresh_out,
    lat_t,
    stale_v,
    conv_w,
    tproj_v,
    qkv_v,
    wout_v,
    ids_v,
    table_v,
    tqkv_v,
    tout_v,
    lat,
    kv_a,
    kv_b,
    halo,
    act,
    stat_out,
    stat_in,
    hidden1,
    wq,
    fresh_v,
    qbuf_a,
    qbuf_b,
    qmask,
    peak,
    acc,
    obuf_a,
    obuf_b,
    lse_a,
    lse_b,
    hid,
    position,
    other,
    twq,
    gathered,
    proj,
    done,
    load_sem,
    halo_send,
    halo_recv,
    stat_send,
    stat_recv,
    ring_send,
    ring_recv,
    part_send,
    part_recv,
    own_sem,
    out_send,
    out_recv,
    back_send,
    back_recv,
):
    block = rows * width
    half = block // 2
    me = lax.axis_index("patch")
    n_patch = lax.axis_size("patch")
    ring = n_patch // 2
    z = lax.rem(me, ring)
    base_z = me - z
    right = base_z + lax.rem(z + 1, ring)
    left = base_z + lax.rem(z + ring - 1, ring)
    partner = lax.rem(me + ring, n_patch)
    frame = lax.axis_index("frame")
    frames = lax.axis_size("frame")
    kv = (kv_a, kv_b)
    qbuf = (qbuf_a, qbuf_b)


    loads = [
        pltpu.make_async_copy(src, dst, load_sem.at[i])
        for i, (src, dst) in enumerate(
            (
                (stale_in, stale_v),
                (lat_in, lat_t),
                (tproj_in, tproj_v),
                (conv_in, conv_w),
                (qkv_in, qkv_v),
                (wout_in, wout_v),
                (ids_in, ids_v),
                (table_in, table_v),
                (tqkv_in, tqkv_v),
                (tout_in, tout_v),
            )
        )
    ]
    (
        load_stale,
        load_lat,
        load_tproj,
        load_conv,
        load_qkv,
        load_wout,
        load_ids,
        load_table,
        load_tqkv,
        load_tout,
    ) = loads

    def ring_copy(stage, direction, i):
        dist = i // 2 + 1
        part = i % 2 if direction == 0 else 1 - i % 2
        window = pl.ds(part * half, half)
        dst_slot = 7 if dist == 4 else 2 * dist - 1 + direction
        src_slot = 0 if dist == 1 else 2 * dist - 3 + direction
        return pltpu.make_async_remote_copy(
            src_ref=kv[stage].at[src_slot, window],
            dst_ref=kv[stage].at[dst_slot, window],
            send_sem=ring_send.at[stage, direction, i],
            recv_sem=ring_recv.at[stage, direction, i],
            device_id={"patch": right if direction == 0 else left},
            device_id_type=MESH,
        )

    def ring_start(stage):
        for i in range(2):
            for direction in range(2):
                ring_copy(stage, direction, i).start()

    def ring_wait(stage, e):
        for direction in range(2):
            ring_copy(stage, direction, e).wait_recv()

    def ring_forward(stage, e):
        for direction in range(2):
            ring_copy(stage, direction, e + 2).start()

    def ring_event(stage, e):
        for direction in range(2):
            ring_copy(stage, direction, e).wait_recv()
            if e + 2 < 7:
                ring_copy(stage, direction, e + 2).start()

    def halo_copy(direction):
        return pltpu.make_async_remote_copy(
            src_ref=lat_t.at[rows - 1 if direction == 0 else 0],
            dst_ref=halo.at[direction],
            send_sem=halo_send.at[direction],
            recv_sem=halo_recv.at[direction],
            device_id={"patch": me + 1 if direction == 0 else me - 1},
            device_id_type=MESH,
        )

    def stat_copy(k):
        return pltpu.make_async_remote_copy(
            src_ref=stat_out,
            dst_ref=stat_in.at[k],
            send_sem=stat_send.at[k],
            recv_sem=stat_recv.at[k],
            device_id={"patch": lax.rem(me + k, n_patch)},
            device_id_type=MESH,
        )

    def part_copy(src, dst, k):
        return pltpu.make_async_remote_copy(
            src_ref=src,
            dst_ref=dst,
            send_sem=part_send.at[k],
            recv_sem=part_recv.at[k],
            device_id={"patch": partner},
            device_id_type=MESH,
        )

    query_copies = [part_copy(qbuf[s].at[0], qbuf[s].at[1], s) for s in range(2)]
    output_copies = [(part_copy(obuf_a.at[0], obuf_a.at[1], 2), part_copy(lse_a.at[0], lse_a.at[1], 3))]
    for c in range(rows):
        window = pl.ds(c * width, width)
        output_copies.append(
            (
                part_copy(obuf_b.at[0, window], obuf_b.at[1, window], 4 + 2 * c),
                part_copy(lse_b.at[0, c], lse_b.at[1, c], 5 + 2 * c),
            )
        )

    def group_rows(g):
        return pl.ds(pl.multiple_of(g * 16, 16), 16)

    per_row = width // 16

    def is_active(f):
        return lax.rem(f, 4) < rows

    def group_of(f):
        return lax.rem(f, 4) * per_row + lax.div(f, 4)

    def out_copy(target):
        return pltpu.make_async_remote_copy(
            src_ref=hid.at[group_rows(group_of(target))],
            dst_ref=gathered.at[group_rows(frame)],
            send_sem=out_send.at[target],
            recv_sem=out_recv.at[frame],
            device_id={"frame": target},
            device_id_type=MESH,
        )

    def back_copy(target):
        return pltpu.make_async_remote_copy(
            src_ref=done.at[group_rows(target)],
            dst_ref=res_out.at[group_rows(group_of(frame))],
            send_sem=back_send.at[target],
            recv_sem=back_recv.at[frame],
            device_id={"frame": target},
            device_id_type=MESH,
        )

    def arrival(source, buffer, rows_of_it, sems):
        return pltpu.make_async_remote_copy(
            src_ref=done.at[pl.ds(0, 16)],
            dst_ref=buffer.at[rows_of_it],
            send_sem=out_send.at[0],
            recv_sem=sems.at[source],
            device_id={"frame": source},
            device_id_type=MESH,
        )


    barrier = pltpu.get_barrier_semaphore()

    def greet_patch(k, carry):
        pl.semaphore_signal(
            barrier,
            inc=1,
            device_id={"patch": lax.rem(me + k, n_patch)},
            device_id_type=MESH,
        )
        return carry

    def greet_frame(k, carry):
        pl.semaphore_signal(
            barrier,
            inc=1,
            device_id={"frame": lax.rem(frame + k, frames)},
            device_id_type=MESH,
        )
        return carry

    lax.fori_loop(1, n_patch, greet_patch, 0)
    lax.fori_loop(1, frames, greet_frame, 0)
    for load in loads:
        load.start()

    low = iota((block, 128), 1) < 64

    def arrange(source, slot):
        kv_a[slot, :, 0:128] = jnp.where(low, source[:, 256:384], source[:, 512:640])
        kv_a[slot, :, 128:256] = source[:, 0:128]
        kv_a[slot, :, 256:384] = source[:, 320:448]
        kv_b[slot, :, 0:128] = source[:, 128:256]
        kv_b[slot, :, 128:256] = source[:, 448:576]

    load_stale.wait()
    arrange(stale_v, 0)
    load_lat.wait()
    for r in range(rows):
        lat[r * width : (r + 1) * width] = lat_t[r].astype(F32).T.astype(BF16)

    pl.semaphore_wait(barrier, n_patch - 1 + frames - 1)
    @pl.when(me < n_patch - 1)
    def _():
        halo_copy(0).start()

    @pl.when(me > 0)
    def _():
        halo_copy(1).start()

    ring_start(0)

    values = lat[...].astype(F32)
    col_sum = jnp.sum(values, axis=0, keepdims=True)
    col_sq = jnp.sum(values * values, axis=0, keepdims=True)
    row8 = iota((8, chans), 0)
    cols = jnp.where(row8 == 0, col_sum, jnp.where(row8 == 1, col_sq, 0.0))
    member = group_of_channel(chans)
    stat_out[...] = dot(cols, member, HIGHEST)

    def send_stat(k, carry):
        stat_copy(k).start()
        return carry

    lax.fori_loop(1, n_patch, send_stat, 0)
    ring_start(1)

    load_tproj.wait()
    lane_c = iota((8, chans), 1)
    half_c = chans // 2
    order = jnp.where(lane_c < half_c, lane_c, lane_c - half_c).astype(F32)
    freqs = jnp.exp(-math.log(10000.0) * order / half_c)
    angles = time_ref[0].astype(F32) * freqs
    emb = jnp.where(lane_c < half_c, jnp.cos(angles), jnp.sin(angles)).astype(BF16)
    bias = dot(emb, tproj_v[...])[0:1]
    load_conv.wait()
    load_qkv.wait()
    wq[...] = jnp.zeros_like(wq)
    wq[:, 0:chans] = qkv_v[:, 0:chans]
    peak[...] = jnp.full(peak.shape, -1e30, F32)
    acc[...] = jnp.zeros(acc.shape, F32)


    def wait_stat(k, carry):
        stat_copy(k).wait_recv()
        return carry

    lax.fori_loop(1, n_patch, wait_stat, 0)
    total = stat_out[...]
    for k in range(1, 16):
        total = total + stat_in[k]
    count = block * (chans // GROUPS) * n_patch
    mean = total[0:1] / count
    var = total[1:2] / count - mean * mean
    rstd = lax.rsqrt(var + 1e-05)
    row8g = iota((8, 128), 0)
    spread = dot_nt(jnp.where(row8g == 0, mean, jnp.where(row8g == 1, rstd, 0.0)), member, HIGHEST)
    mean_c, rstd_c = spread[0:1], spread[1:2]

    def activate(x):
        normed = (x.astype(F32) - mean_c) * rstd_c
        return (normed / (1.0 + jnp.exp(-normed))).astype(BF16)

    act[width : width + block] = activate(lat[...])

    @pl.when(me > 0)
    def _():
        halo_copy(0).wait_recv()
        act[0:width] = activate(halo[0].astype(F32).T)

    @pl.when(me == 0)
    def _():
        act[0:width] = jnp.zeros((width, chans), BF16)

    @pl.when(me < n_patch - 1)
    def _():
        halo_copy(1).wait_recv()
        act[width + block :] = activate(halo[1].astype(F32).T)

    @pl.when(me == n_patch - 1)
    def _():
        act[width + block :] = jnp.zeros((width, chans), BF16)

    ring_event(0, 0)


    column = iota((block, chans), 0) & (width - 1)

    def conv_column(step):
        out = dot(act[0:block], conv_w[0, step])
        out = out + dot(act[width : width + block], conv_w[1, step])
        return out + dot(act[2 * width : 2 * width + block], conv_w[2, step])

    conv = conv_column(1)
    conv = conv + jnp.where(column == 0, 0.0, pltpu.roll(conv_column(0), 1, 0))
    ring_event(0, 1)
    conv = conv + jnp.where(column == width - 1, 0.0, pltpu.roll(conv_column(2), block - 1, 0))
    h1 = lat[...].astype(F32) + conv + bias
    hidden1[...] = h1
    norm1 = layer_norm(h1).astype(BF16)
    queries = dot(norm1, wq[...]) * (LOG2E / 8.0)
    low_half = iota((half, 128), 1) < 64
    qbuf_a[0, 0:block] = queries[:, 0:128].astype(BF16)
    folded = jnp.where(
        low_half, queries[0:half, 256:384], pltpu.roll(queries[half:, 256:384], 64, 1)
    )
    qbuf_a[0, block:] = folded.astype(BF16)
    query_copies[0].start()
    qbuf_b[0] = queries[:, 128:256].astype(BF16)
    query_copies[1].start()
    ring_event(1, 0)
    ring_event(1, 1)
    fresh_v[...] = dot(norm1, qkv_v[:, chans:]).astype(BF16)
    store_fresh = pltpu.make_async_copy(fresh_v, fresh_out, own_sem.at[2])
    store_fresh.start()
    arrange(fresh_v, FRESH)

    def mask_queries(stage, which):
        def keep(tile, lanes):
            return jnp.where(lanes, tile, jnp.zeros_like(tile))

        if stage == 0:
            tile = qbuf_a[which, 0:block]
            qmask[which, 0] = keep(tile, low)
            qmask[which, 1] = keep(tile, ~low)
            tile = qbuf_a[which, block:].astype(F32)
            qmask[which, 2, 0:half] = jnp.where(low_half, tile, 0.0).astype(BF16)
            tile = pltpu.roll(tile, 64, 1)
            qmask[which, 2, half:] = jnp.where(low_half, tile, 0.0).astype(BF16)
        else:
            tile = qbuf_b[which]
            qmask[which, 3] = keep(tile, low)
            qmask[which, 4] = keep(tile, ~low)

    mask_queries(0, 0)
    mask_queries(1, 0)


    def attend(stage, which, slot, slots):
        heads = STAGES[stage]
        keys = slots * block
        low_keys = iota((keys, 128), 1) < 64

        def tile_of(t):
            return kv[stage][pl.ds(slot, slots), :, t * 128 : t * 128 + 128].reshape(keys, 128)

        def scores_of(j):
            return dot_nt(qmask[which, FIRST[stage] + j], tile_of(heads[j][0]))

        accs = [acc[which, FIRST[stage] + j] for j in range(len(heads))]
        peaks = [peak[which, FIRST[stage] + j] for j in range(len(heads))]
        scores = scores_of(0)
        results = []
        for j, (_, vt, in_low) in enumerate(heads):
            following = scores_of(j + 1) if j + 1 < len(heads) else None
            top = jnp.maximum(peaks[j], jnp.max(scores, axis=1, keepdims=True))
            weights = jnp.exp2(scores - jnp.concatenate([top] * (keys // 128), axis=1))
            vals = tile_of(vt)
            vals = jnp.where(low_keys if in_low else ~low_keys, vals, jnp.ones_like(vals))
            scale = jnp.exp2(peaks[j] - top)
            results.append((accs[j] * scale + dot(weights.astype(BF16), vals), top))
            scores = following
        for j, (new_acc, top) in enumerate(results):
            acc[which, FIRST[stage] + j] = new_acc
            peak[which, FIRST[stage] + j] = top

    lane = iota((block, 128), 1)

    def settle(which, stage, j, window):
        a = acc[which, FIRST[stage] + j, window]
        turned = pltpu.roll(a, 64, 1)
        mine = (iota(a.shape, 1) >= 64) if STAGES[stage][j][2] else (iota(a.shape, 1) < 64)
        sums = jnp.where(mine, a, turned)
        return a / sums, peak[which, FIRST[stage] + j, window] + jnp.log2(sums)

    def part_of(c):
        if c is None:
            return 0, slice(0, block), output_copies[0]
        return 1, slice(c * width, (c + 1) * width), output_copies[1 + c]

    def finish_partner(c=None):
        stage, window, copies = part_of(c)
        outs = [settle(1, stage, j, window) for j in range(len(STAGES[stage]))]
        count_rows = window.stop - window.start
        low_rows = iota((count_rows, 128), 1) < 64
        pair = jnp.where(low_rows, outs[0][0], outs[1][0]).astype(BF16)
        if stage == 0:
            obuf_a[0, 0:block] = pair
            out = outs[2][0]
            folded = jnp.where(low_half, pltpu.roll(out[half:], 64, 1), out[0:half])
            obuf_a[0, block:] = folded.astype(BF16)
        else:
            obuf_b[0, window] = pair
        copies[0].start()
        lane = iota((count_rows, 128), 1)
        sums = jnp.zeros((count_rows, 128), F32)
        for j, (_, lse) in enumerate(outs):
            sums = jnp.where(lane == j, lse, sums)
        if stage == 0:
            lse_a[0] = sums.T[0:8]
        else:
            lse_b[0, c] = sums.T[0:8]
        copies[1].start()

    def own_part(c=None):
        stage, window, _ = part_of(c)
        return [settle(0, stage, j, window) for j in range(len(STAGES[stage]))]

    def joined(own, c=None):
        stage, window, copies = part_of(c)
        for copy in copies:
            copy.wait_recv()
        sent = lse_a[1] if stage == 0 else lse_b[1, c]
        there = jnp.concatenate([sent, jnp.zeros((120, sent.shape[1]), F32)], axis=0).T
        outs = []
        for j, (out, lse) in enumerate(own):
            if stage == 1:
                out_there = obuf_b[1, window].astype(F32)
            elif j < 2:
                out_there = obuf_a[1, 0:block].astype(F32)
            else:
                folded = obuf_a[1, block:].astype(F32)
                out_there = jnp.concatenate([folded, pltpu.roll(folded, 64, 1)], axis=0)
            lse_there = there[:, j : j + 1]
            top = jnp.maximum(lse, lse_there)
            weight = jnp.exp2(lse - top)
            weight_there = jnp.exp2(lse_there - top)
            mixed = out * weight + out_there * weight_there
            outs.append(mixed / (weight + weight_there))
        return outs

    everything = frames * 16

    def prepare_temporal():
        load_ids.wait()
        load_table.wait()
        load_tqkv.wait()
        npos = table_v.shape[0]
        picked = jnp.where(iota((npos, frames), 0) == ids_v[...], 1.0, 0.0).astype(BF16)
        repeat = jnp.where(
            (iota((everything, frames), 0) >> 4) == iota((everything, frames), 1), 1.0, 0.0
        ).astype(BF16)
        onehot = dot_nt(repeat, picked).astype(BF16)
        position[...] = dot(onehot, table_v[...])
        other[...] = jnp.where(
            (iota((everything, everything), 0) & 15) == (iota((everything, everything), 1) & 15),
            0.0,
            -1e30,
        )
        twq[...] = jnp.zeros_like(twq)
        for part in range(3):
            twq[:, part * 384 : part * 384 + chans] = tqkv_v[:, part * chans : (part + 1) * chans]

    before = {
        1: lambda: ring_event(0, 2),
        4: lambda: ring_event(0, 3),
        5: lambda: (ring_wait(1, 2), ring_wait(1, 3)),
        6: lambda: (
            prepare_temporal(),
            ring_event(0, 4),
            ring_forward(1, 2),
            ring_forward(1, 3),
            query_copies[0].wait_recv(),
            mask_queries(0, 1),
        ),
        9: lambda: ring_event(0, 5),
        10: lambda: (query_copies[1].wait_recv(), mask_queries(1, 1)),
        12: lambda: ring_event(0, 6),
        13: lambda: (finish_partner(), ring_event(1, 4)),
        15: lambda: ring_event(1, 5),
        17: lambda: ring_event(1, 6),
        18: lambda: [finish_partner(c) for c in range(rows)],
    }

    def step(i, carry):
        for k, actions in before.items():

            @pl.when(i == k)
            def _():
                actions()

        which = lookup(i, [s[1] for s in STEPS])
        slot = lookup(i, [s[2] for s in STEPS])
        kind = lookup(i, [2 * s[0] + s[3] - 1 for s in STEPS])
        for stage in range(2):
            for slots in (1, 2):
                pl.when(kind == 2 * stage + slots - 1)(
                    functools.partial(attend, stage, which, slot, slots)
                )
        return carry

    lax.fori_loop(0, len(STEPS), step, 0)

    load_wout.wait()
    load_tout.wait()


    first = joined(own_part())
    pair = jnp.where(low, first[0], first[1]).astype(BF16)
    last = pltpu.roll(first[2], 64, 1)[:, 0:64].astype(BF16)
    hidden1[...] = (
        hidden1[...] + dot(pair, wout_v[0:128]) + dot(last, wout_v[256:chans])
    )
    quarter = frames // 4
    low_row = iota((width, 128), 1) < 64
    own_rows = [own_part(c) for c in range(rows)]
    for c in range(rows):
        second = joined(own_rows[c], c)
        window = slice(c * width, (c + 1) * width)
        pair = jnp.where(low_row, second[0], second[1]).astype(BF16)
        hid[window] = (hidden1[window] + dot(pair, wout_v[128:256])).astype(BF16)

        def send_out(k, carry, c=c):
            target = lax.rem(lax.div(frame, 4) + k, quarter) * 4 + c

            @pl.when(target != frame)
            def _():
                out_copy(target).start()

            return carry

        lax.fori_loop(0, quarter, send_out, 0)


    @pl.when(is_active(frame))
    def _():
        mine = group_rows(group_of(frame))
        keep = pltpu.make_async_copy(hid.at[mine], gathered.at[group_rows(frame)], own_sem.at[0])
        keep.start()
        keep.wait()

        def wait_out(k, carry):
            source = lax.rem(frame + k, frames)
            arrival(source, gathered, group_rows(source), out_recv).wait_recv()
            return carry

        lax.fori_loop(1, frames, wait_out, 0)

        inputs = gathered[...].astype(F32)
        norm2 = layer_norm(inputs + position[...]).astype(BF16)
        proj[:, 0:384] = (dot(norm2, twq[:, 0:384]) * (LOG2E / 8.0)).astype(BF16)
        proj[:, 384:] = dot(norm2, twq[:, 384:]).astype(BF16)

        low_t = iota((everything, 128), 1) < 64
        upper = everything // 2

        def lanes_of(h):
            return low_t if h % 2 == 0 else ~low_t

        def masked(h, rows_of_it, first_lane, fill):
            tile = proj[rows_of_it, first_lane + (h // 2) * 128 : first_lane + (h // 2) * 128 + 128]
            return jnp.where(lanes_of(h)[0 : tile.shape[0]], tile, fill(tile))

        def send_half(part):
            window = slice(part * upper, (part + 1) * upper)

            def scores_t(h):
                keys = proj[:, 384 + (h // 2) * 128 : 384 + (h // 2) * 128 + 128]
                return dot_nt(masked(h, window, 0, jnp.zeros_like), keys)

            low_h = low_t[0:upper]
            outs = []
            scores = scores_t(0)
            for h in range(HEADS):
                following = scores_t(h + 1) if h + 1 < HEADS else None
                scores = scores + other[window]
                weights = jnp.exp2(scores - jnp.max(scores, axis=1, keepdims=True)).astype(BF16)
                mixed = dot(weights, masked(h, slice(0, everything), 768, jnp.ones_like))
                outs.append(mixed / pltpu.roll(mixed, 64, 1))
                scores = following
            temporal = jnp.concatenate(
                [
                    jnp.where(low_h, outs[0], outs[1]).astype(BF16),
                    jnp.where(low_h, outs[2], outs[3]).astype(BF16),
                    outs[4][:, 0:64].astype(BF16),
                ],
                axis=1,
            )
            done[window] = (
                gathered[window].astype(F32) + dot(temporal, tout_v[...])
            ).astype(BF16)

            def send_back(k, carry):
                target = part * (frames // 2) + lax.rem(frame + k, frames // 2)

                @pl.when(target != frame)
                def _():
                    back_copy(target).start()

                return carry

            lax.fori_loop(0, frames // 2, send_back, 0)

        send_half(0)
        send_half(1)
        put = pltpu.make_async_copy(done.at[group_rows(frame)], res_out.at[mine], own_sem.at[1])
        put.start()
        put.wait()

    def wait_stat_send(k, carry):
        stat_copy(k).wait_send()
        return carry

    lax.fori_loop(1, n_patch, wait_stat_send, 0)

    @pl.when(me < n_patch - 1)
    def _():
        halo_copy(0).wait_send()

    @pl.when(me > 0)
    def _():
        halo_copy(1).wait_send()

    for stage in range(2):
        for i in range(7):
            for direction in range(2):
                ring_copy(stage, direction, i).wait_send()
        query_copies[stage].wait_send()
    store_fresh.wait()

    for copies in output_copies:
        for copy in copies:
            copy.wait_send()

    def wait_out_send(k, carry):
        target = lax.rem(frame + k, frames)

        @pl.when(is_active(target))
        def _():
            out_copy(target).wait_send()

        return carry

    lax.fori_loop(1, frames, wait_out_send, 0)

    def wait_back(k, carry):
        source = lax.rem(frame + k, frames)

        @pl.when(is_active(source))
        def _():
            arrival(source, res_out, group_rows(group_of(source)), back_recv).wait_recv()

        return carry

    lax.fori_loop(1, frames, wait_back, 0)
    @pl.when(is_active(frame))
    def _():
        def wait_back_send(k, carry):
            back_copy(lax.rem(frame + k, frames)).wait_send()
            return carry

        lax.fori_loop(1, frames, wait_back_send, 0)


def emit_kernel(res_in, fresh_in, res_out, fresh_out, res_v, res_t, fresh_v, sems):
    rows, _, width = res_out.shape
    parts = [pl.ds(width * i, width) for i in range(rows)]

    def copies(k, src, dst):
        return pltpu.make_async_copy(src, dst, sems.at[k])

    res_loads = [copies(i, res_in.at[p], res_v.at[p]) for i, p in enumerate(parts)]
    fresh_loads = [copies(3 + i, fresh_in.at[p], fresh_v.at[p]) for i, p in enumerate(parts)]
    res_stores = [copies(6 + i, res_t.at[i], res_out.at[i]) for i in range(rows)]
    fresh_stores = [copies(9 + i, fresh_v.at[p], fresh_out.at[p]) for i, p in enumerate(parts)]
    for copy in res_loads + fresh_loads:
        copy.start()
    for i in range(rows):
        res_loads[i].wait()
        res_t[i] = res_v[parts[i]].astype(F32).T.astype(BF16)
        res_stores[i].start()
    for i in range(rows):
        fresh_loads[i].wait()
        fresh_stores[i].start()
    for copy in res_stores + fresh_stores:
        copy.wait()


def body(
    latents,
    stale_kv,
    frame_ids,
    timestep,
    conv_weight,
    time_proj,
    spatial_qkv,
    spatial_out,
    temporal_qkv,
    temporal_out,
    frame_table,
):
    rows, width, chans = latents.shape[1:]
    block = rows * width
    frames = frame_ids.shape[0]
    npos = frame_table.shape[0]
    dma = pltpu.SemaphoreType.DMA
    vmem = pltpu.VMEM
    anywhere = pl.BlockSpec(memory_space=pl.ANY)
    result, fresh = pl.pallas_call(
        functools.partial(kernel, rows, width, chans),
        out_shape=(
            jax.ShapeDtypeStruct((block, chans), BF16),
            jax.ShapeDtypeStruct((block, 2 * chans), BF16),
        ),
        in_specs=[anywhere, anywhere, pl.BlockSpec(memory_space=pltpu.SMEM)] + [anywhere] * 8,
        out_specs=(anywhere, anywhere),
        scratch_shapes=[
            vmem((rows, chans, width), BF16),
            vmem((block, 2 * chans), BF16),
            vmem((3, 3, chans, chans), BF16),
            vmem((chans, chans), BF16),
            vmem((chans, 3 * chans), BF16),
            vmem((chans, chans), BF16),
            vmem((1, frames), jnp.int32),
            vmem((npos, chans), BF16),
            vmem((chans, 3 * chans), BF16),
            vmem((chans, chans), BF16),
            vmem((block, chans), BF16),
            vmem((9, block, 384), BF16),
            vmem((9, block, 256), BF16),
            vmem((2, chans, width), BF16),
            vmem((block + 2 * width, chans), BF16),
            vmem((8, 128), F32),
            vmem((16, 8, 128), F32),
            vmem((block, chans), F32),
            vmem((chans, 384), BF16),
            vmem((block, 2 * chans), BF16),
            vmem((2, block + block // 2, 128), BF16),
            vmem((2, block, 128), BF16),
            vmem((2, HEADS, block, 128), BF16),
            vmem((2, HEADS, block, 128), F32),
            vmem((2, HEADS, block, 128), F32),
            vmem((2, block + block // 2, 128), BF16),
            vmem((2, block, 128), BF16),
            vmem((2, 8, block), F32),
            vmem((2, rows, 8, width), F32),
            vmem((block, chans), BF16),
            vmem((frames * 16, chans), F32),
            vmem((frames * 16, frames * 16), F32),
            vmem((chans, 3 * 384), BF16),
            vmem((frames * 16, chans), BF16),
            vmem((frames * 16, 3 * 384), BF16),
            vmem((frames * 16, chans), BF16),
            dma((10,)),
            dma((2,)),
            dma((2,)),
            dma((16,)),
            dma((16,)),
            dma((2, 2, 7)),
            dma((2, 2, 7)),
            dma((4 + 2 * rows,)),
            dma((4 + 2 * rows,)),
            dma((4,)),
            dma((frames,)),
            dma((frames,)),
            dma((frames,)),
            dma((frames,)),
        ],
        compiler_params=pltpu.CompilerParams(
            collective_id=0, has_side_effects=True, vmem_limit_bytes=60 * 1024 * 1024
        ),
        name="layer",
    )(
        jnp.transpose(latents, (0, 1, 3, 2)).reshape(rows, chans, width),
        stale_kv.reshape(block, 2 * chans),
        timestep,
        conv_weight,
        time_proj,
        spatial_qkv,
        spatial_out,
        frame_ids.reshape(1, frames),
        frame_table,
        temporal_qkv,
        temporal_out,
    )
    result, fresh = pl.pallas_call(
        emit_kernel,
        out_shape=(
            jax.ShapeDtypeStruct((rows, chans, width), BF16),
            jax.ShapeDtypeStruct(fresh.shape, BF16),
        ),
        in_specs=[anywhere] * 2,
        out_specs=(anywhere, anywhere),
        scratch_shapes=[
            vmem(result.shape, BF16),
            vmem((rows, chans, width), BF16),
            vmem(fresh.shape, BF16),
            dma((12,)),
        ],
        compiler_params=pltpu.CompilerParams(vmem_limit_bytes=62 * 1024 * 1024),
        name="emit",
    )(result, fresh)
    result = jnp.transpose(result.reshape(1, rows, chans, width), (0, 1, 3, 2))
    return result, fresh.reshape(stale_kv.shape)


def solution(mesh):
    return jax.shard_map(
        body,
        mesh=mesh,
        in_specs=(
            P("frame", "patch", None, None),
            P("frame", "patch", None, None),
            P(),
            P(),
            P(),
            P(),
            P(),
            P(),
            P(),
            P(),
            P(),
        ),
        out_specs=(P("frame", "patch", None, None), P("frame", "patch", None, None)),
        check_vma=False,
    )
```
